128 devices in a mesh: ka: 8 (over y_lo, x), pb: 16 (over z, y_hi, core).
Axes of the slice: x: 4, y: 4 (y_hi: 2, y_lo: 2; y = y_hi * 2 + y_lo), z: 4, core: 2. Of those that a mesh axis runs over, the one named last changes fastest.
Arguments:
- occupation: bfloat16 [80, 4, 6400], P('ka'), may hold values from 0.049804688 to 1
- q_offsets: int32 [16, 3], P('pb'), may hold values from 0 to 79
- coupling: bfloat16 [16, 2, 200, 96], P('pb'), may hold values from -0.4375 to 0.4375
- window_bins: int32 [16, 16], P('pb'), may hold values from 0 to 31
- lorentz_table: float32 [32, 6], replicated, may hold values from 0.1 to 1
- lattice: int32 [3, 200], replicated, may hold values from -6 to 6
Outputs:
- collision: float32 [80, 4, 6400], P('ka', None, 'pb')
The draws below stay inside these ranges and needn't reach their ends.
All inputs are finite; a program needn't handle non-finite values.
Results may differ from the reference program's by a relative error of at most 0.0003.
Values may be sent and summed in bfloat16 or wider, within the bound.
No kernel may reach another device: no remote copies, remote signals or barrier semaphores. Data moves between devices by JAX's collectives and lax.ppermute only.
A program may use at most 128 MiB of HBM per device.

```python
import math
import jax
import jax.numpy as jnp
from jax import lax

KX = 80
KY = 80
KZ = 80
NB = 4
NM = 6
NR = 200
CH = 96
NBIN = 32
Q = 16


def set_ends(entries, own_key, low, high):
    place = [jax.random.randint(jax.random.fold_in(own_key, axis), (), 0, length) for axis, length in enumerate(entries.shape)]
    longest = entries.shape.index(max(entries.shape))
    beside = place[:longest] + [(place[longest] + 1) % entries.shape[longest]] + place[longest + 1:]
    return entries.at[tuple(place)].set(low).at[tuple(beside)].set(high)


def block_levels(stream_key, extent, pieces, least, largest):
    gain, own = 1.0, jax.random.fold_in(stream_key, 6)
    for position, parts in pieces:
        steps = jnp.exp(jax.random.uniform(jax.random.fold_in(own, position), (parts,), jnp.float32, least / len(pieces), largest / len(pieces)))
        gain = gain * jnp.repeat(steps, extent[position] // parts).reshape([-1 if axis == position else 1 for axis in range(len(extent))])
    return gain


def normal_values(key, shape, width, limit, split=(), kind=jnp.bfloat16):
    array = width * jax.random.normal(key, shape, jnp.float32)
    if split:
        array = array * block_levels(key, shape, split, -0.22, 0.18)
    return jnp.clip(array, -limit, limit).astype(kind)


def setup_inputs(seed: int = 0) -> dict:
    key_list = jax.random.split(jax.random.key(seed), 7)
    return {
        "occupation": jnp.clip(jnp.exp(math.log(1.0) - 2.9996462 * jax.random.uniform(key_list[0], (KZ, NB, KX * KY), jnp.float32) ** block_levels(key_list[0], (KZ, NB, KX * KY), ((0, 8),), -0.2, 0.2)), 0.049804688, 1.0).astype(jnp.bfloat16),
        "q_offsets": set_ends(jax.random.randint(key_list[1], (Q, 3), 0, min(KX, KY, KZ)), jax.random.fold_in(key_list[1], 1), 0, (min(KX, KY, KZ)) - 1).astype(jnp.int32),
        "coupling": normal_values(key_list[2], (Q, 2, NR, CH), NR ** -0.5, 0.4375, ((0, 16),)),
        "window_bins": set_ends(jax.random.randint(key_list[3], (Q, NB * NB), 0, NBIN), jax.random.fold_in(key_list[3], 1), 0, NBIN - 1).astype(jnp.int32),
        "lorentz_table": jnp.clip(jnp.exp(jax.random.uniform(key_list[4], (NBIN, NM), jnp.float32, math.log(0.1), math.log(1.0))), 0.1, 1.0),
        "lattice": set_ends(jax.random.randint(key_list[5], (3, NR), -6, 7), jax.random.fold_in(key_list[5], 1), -6, 6).astype(jnp.int32),
    }


def phase_rows(plane_z, lattice, kpt_x, kpt_y, grid_depth):
    first_term = ((kpt_x[None, :] * lattice[0][:, None]) % KX) * (KY * grid_depth)
    second_term = ((kpt_y[None, :] * lattice[1][:, None]) % KY) * (KX * grid_depth)
    third_term = ((plane_z * lattice[2]) % grid_depth) * (KX * KY)
    flat_index = first_term + second_term + third_term[:, None]
    angles = flat_index.astype(jnp.float32) * (2.0 * math.pi / (KX * KY * grid_depth))
    return jnp.concatenate([jnp.cos(angles), jnp.sin(angles)], axis=0).astype(jnp.bfloat16)


def coupling_rows(q_block):
    upper_half = jnp.concatenate([q_block[0], q_block[1]], axis=1)
    lower_half = jnp.concatenate([-q_block[1], q_block[0]], axis=1)
    return jnp.concatenate([upper_half, lower_half], axis=0).T


def channel_weights(bins_row, lorentz_table):
    levels = jnp.arange(lorentz_table.shape[0], dtype=jnp.int32)
    onehot = (bins_row[:, None] == levels[None, :]).astype(jnp.float32)
    table = jnp.dot(onehot, lorentz_table, precision=lax.Precision.HIGHEST, preferred_element_type=jnp.float32)
    return table.reshape(-1)


def plane_term(phases, mat_t, weight, own_occ, arrived):
    couple = jnp.dot(mat_t, phases, preferred_element_type=jnp.float32)
    channels = weight.shape[0]
    squared = couple[:channels] * couple[:channels] + couple[channels:] * couple[channels:]
    strength = (squared * weight[:, None]).reshape(NB, NB, NM, -1).sum(axis=2)
    outgoing = strength.sum(axis=1)
    incoming = jnp.sum(strength * arrived.astype(jnp.float32)[None, :, :], axis=1)
    return incoming - outgoing * own_occ.astype(jnp.float32)


def reference(occupation, q_offsets, coupling, window_bins, lorentz_table, lattice):
    plane_size = KX * KY
    flat_k = jnp.arange(plane_size, dtype=jnp.int32)
    kpt_x = flat_k // KY
    kpt_y = flat_k % KY
    occ_grid = occupation.reshape(KZ, NB, KX, KY)
    shifted_all = jnp.stack([
        jnp.roll(occ_grid, (-q_offsets[q_pos, 2], -q_offsets[q_pos, 0], -q_offsets[q_pos, 1]), axis=(0, 2, 3))
        for q_pos in range(Q)]).reshape(Q, KZ, NB, plane_size)
    shifted_all = jnp.swapaxes(shifted_all, 0, 1)
    q_mats = jnp.stack([coupling_rows(coupling[q_pos]) for q_pos in range(Q)])
    q_weights = jnp.stack([channel_weights(window_bins[q_pos], lorentz_table) for q_pos in range(Q)])

    def one_plane(inputs):
        plane_z, own_occ, shifted = inputs
        phases = phase_rows(plane_z, lattice, kpt_x, kpt_y, KZ)

        def add_q(running, q_item):
            mat_t, weight, arrived = q_item
            return running + plane_term(phases, mat_t, weight, own_occ, arrived), None

        return lax.scan(add_q, jnp.zeros((NB, plane_size), jnp.float32), (q_mats, q_weights, shifted))[0]

    q_terms = lax.map(one_plane, (jnp.arange(KZ, dtype=jnp.int32), occupation, shifted_all))
    return q_terms * (1.0 / (Q * NM))
```

```python
import math

import jax
import jax.numpy as jnp
from jax import lax
from jax.experimental import pallas as pl
from jax.experimental.pallas import tpu as pltpu
from jax.sharding import PartitionSpec as P

KX = 80
KY = 80
KZ = 80
NB = 4
NM = 6
NR = 200
RP = 208
RW = 256
CH = 96
NBIN = 32
QG = 8
PLANES = 10
ROWS = 5
SHARE = ROWS * KY
PAY = 2 * RP + 16
FRONT = 128
BACK = 512
VLANES = FRONT + KX * KY + BACK
WIN = 640
VMEM_LIMIT = 50 * 1024 * 1024


def phase_kernel(ac_ref, as_ref, bc_ref, bs_ref, out_ref):
    bc = bc_ref[...]
    bs = bs_ref[...]
    for row in range(ROWS):
        ac = ac_ref[0, row : row + 1, :]
        an = as_ref[0, row : row + 1, :]
        cosine = ac * bc - an * bs
        sine = an * bc + ac * bs
        out_ref[row * KY : (row + 1) * KY, :RW] = cosine.astype(jnp.bfloat16)
        out_ref[row * KY : (row + 1) * KY, RW:] = sine.astype(jnp.bfloat16)


def make_phases(ac, an, bc, bs):
    plane = pl.BlockSpec((1, ROWS, RW), lambda i: (i, 0, 0))
    whole = pl.BlockSpec((KY, RW), lambda i: (0, 0))
    return pl.pallas_call(
        phase_kernel,
        grid=(PLANES,),
        in_specs=[plane, plane, whole, whole],
        out_specs=pl.BlockSpec((SHARE, 2 * RW), lambda i: (i, 0)),
        out_shape=jax.ShapeDtypeStruct((PLANES * SHARE, 2 * RW), jnp.bfloat16),
        cost_estimate=pl.CostEstimate(flops=10_000_000, bytes_accessed=5_000_000, transcendentals=0),
        name="phases",
    )(ac, an, bc, bs)


def strength_kernel(table_ref, p0, p1, p2, p3, ph_ref, s_ref, off_ref, g_ref, w_ref):
    @pl.when(pl.program_id(0) == 0)
    def _():
        channel = lax.broadcasted_iota(jnp.int32, (CH, NM * 128), 0)
        column = lax.broadcasted_iota(jnp.int32, (CH, NM * 128), 1)
        pair = (channel * 43) >> 8
        target = (channel - NM * pair) * 128 + pair
        total = None
        for slot in range(QG):
            ref = (p0, p1, p2, p3)[slot // 2]
            block = ref[(slot % 2) * PAY : (slot % 2 + 1) * PAY, :]
            place = jnp.where(column - 16 * slot == target, 1.0, 0.0).astype(jnp.bfloat16)
            part = jnp.dot(block, place, preferred_element_type=jnp.float32)
            total = part if total is None else total + part
        real = total[:RP].astype(jnp.bfloat16)
        imag = total[RP : 2 * RP].astype(jnp.bfloat16)
        minus = (-total[RP : 2 * RP]).astype(jnp.bfloat16)
        zeros = jnp.zeros((RW - RP, 2 * NM * 128), jnp.bfloat16)
        g_ref[RP:RW, :] = zeros
        g_ref[RW + RP :, :] = zeros
        for mode in range(NM):
            lanes = slice(mode * 128, (mode + 1) * 128)
            left = slice(mode * 256, mode * 256 + 128)
            right = slice(mode * 256 + 128, mode * 256 + 256)
            g_ref[:RP, left] = real[:, lanes]
            g_ref[:RP, right] = imag[:, lanes]
            g_ref[RW : RW + RP, left] = minus[:, lanes]
            g_ref[RW : RW + RP, right] = real[:, lanes]
        bins = total[2 * RP : 2 * RP + 1, :128]
        off_ref[...] = jnp.broadcast_to(total[2 * RP : 2 * RP + 1, 128:256], (8, 128)).astype(jnp.int32)
        for mode in range(NM):
            weight = jnp.zeros((1, 128), jnp.float32)
            for level in range(NBIN):
                weight = jnp.where(bins == float(level), table_ref[level, mode], weight)
            w_ref[mode : mode + 1, :] = weight

    phases = ph_ref[...]
    acc = None
    for mode in range(NM):
        couple = jnp.dot(phases, g_ref[:, mode * 256 : (mode + 1) * 256], preferred_element_type=jnp.float32)
        re = couple[:, :128]
        im = couple[:, 128:]
        term = (re * re + im * im) * w_ref[mode : mode + 1, :]
        acc = term if acc is None else acc + term
    s_ref[...] = acc


def strengths(table, pays, phases):
    vmem = pl.BlockSpec((2 * PAY, CH), lambda i: (0, 0))
    return pl.pallas_call(
        strength_kernel,
        grid=(PLANES,),
        in_specs=[pl.BlockSpec(memory_space=pltpu.SMEM)] + [vmem] * 4 + [pl.BlockSpec((SHARE, 2 * RW), lambda i: (i, 0))],
        out_specs=[pl.BlockSpec((SHARE, 128), lambda i: (i, 0)), pl.BlockSpec((8, 128), lambda i: (0, 0))],
        out_shape=[jax.ShapeDtypeStruct((PLANES * SHARE, 128), jnp.float32), jax.ShapeDtypeStruct((8, 128), jnp.int32)],
        scratch_shapes=[pltpu.VMEM((2 * RW, 2 * NM * 128), jnp.bfloat16), pltpu.VMEM((8, 128), jnp.float32)],
        compiler_params=pltpu.CompilerParams(vmem_limit_bytes=VMEM_LIMIT),
        cost_estimate=pl.CostEstimate(flops=6_300_000_000, bytes_accessed=8_000_000, transcendentals=0),
        name="strengths",
    )(table, *pays, phases)


def final_kernel(where_ref, off_a, off_b, own, *refs):
    parts = refs[:14]
    sa_ref, sb_ref, out_ref, v_ref, arr_ref, sem = refs[14:]
    step = pl.program_id(0)
    slab = where_ref[0]
    core = where_ref[1]
    share = where_ref[2]

    @pl.when(step == 0)
    def _():
        copies = []

        def bring(src, plane, count):
            dst = v_ref.at[pl.ds(plane, count)]
            copies.append(pltpu.make_async_copy(src, dst.at[:, :, FRONT : FRONT + KX * KY], sem.at[len(copies)]))
            copies.append(pltpu.make_async_copy(src.at[:, :, :BACK], dst.at[:, :, FRONT + KX * KY :], sem.at[len(copies)]))
            copies.append(pltpu.make_async_copy(src.at[:, :, KX * KY - FRONT :], dst.at[:, :, :FRONT], sem.at[len(copies)]))

        bring(own, slab * PLANES, PLANES)
        for index in range(7):
            source = where_ref[3 + index]
            bring(parts[index], source * PLANES + core * (PLANES // 2), PLANES // 2)
            bring(parts[7 + index], source * PLANES + (1 - core) * (PLANES // 2), PLANES // 2)
        for copy in copies:
            copy.start()
        for copy in copies:
            copy.wait()

    lane = lax.broadcasted_iota(jnp.int32, (NB, 512), 1)
    ky = lax.rem(lane, KY)
    for slot in range(2 * QG):
        off = (off_a, off_b)[slot // QG]
        base = (slot % QG) * 16
        qx = off[0, base]
        qy = off[0, base + 1]
        qz = off[0, base + 2]
        plane = lax.rem(slab * PLANES + step + qz, KZ)
        first = lax.rem(share * ROWS + qx, KX) * KY
        start = first + qy + (FRONT - KY)
        aligned = pl.multiple_of((start >> 7) * 128, 128)
        window = v_ref[plane, :, pl.ds(aligned, WIN)].astype(jnp.float32)
        late = pltpu.roll(window, lax.rem(WIN - (start - aligned), WIN), 1)
        early = pltpu.roll(late, WIN - KY, 1)
        arr_ref[NB * slot : NB * (slot + 1), :] = jnp.where(ky + qy < KY, early[:, :512], late[:, :512])
    window = v_ref[slab * PLANES + step, :, pl.ds(pl.multiple_of(((share * SHARE + FRONT) >> 7) * 128, 128), WIN)].astype(jnp.float32)
    rest = lax.rem(share * SHARE, 128)
    occ = pltpu.roll(window, lax.rem(WIN - rest, WIN), 1)
    arr_ref[64:68, :] = occ[:, :512]
    arr_ref[68:80, :] = jnp.zeros((12, 512), jnp.float32)
    arrived = arr_ref[...].astype(jnp.bfloat16)
    row = lax.broadcasted_iota(jnp.int32, (80, 256), 0)
    col = lax.broadcasted_iota(jnp.int32, (80, 256), 1)
    gain = (row < 64) & (row >> 2 == col >> 4) & (row & 3 == col & 3)
    loss = (row >= 64) & (row - 64 == (col >> 2) & 3)
    spread = (jnp.where(gain, 1.0, 0.0) - jnp.where(loss, 1.0, 0.0)).astype(jnp.bfloat16)
    diff = lax.dot_general(arrived, spread, (((0,), (0,)), ((), ())), preferred_element_type=jnp.float32)[:SHARE]
    term = sa_ref[...] * diff[:, :128] + sb_ref[...] * diff[:, 128:]
    band = lax.broadcasted_iota(jnp.int32, (8, 128), 0)
    lane8 = lax.broadcasted_iota(jnp.int32, (8, 128), 1)
    pick = jnp.where((lane8 >> 2) & 3 == band, 1.0, 0.0).astype(jnp.bfloat16)
    result = None
    for _ in range(3):
        piece = term.astype(jnp.bfloat16)
        term = term - piece.astype(jnp.float32)
        got = lax.dot_general(pick, piece, (((1,), (1,)), ((), ())), preferred_element_type=jnp.float32)
        result = got if result is None else result + got
    out_ref[0] = result[:NB] * (1.0 / (2 * QG * NM))


def contract(where, off_a, off_b, own, parts, s_a, s_b):
    smem = pl.BlockSpec(memory_space=pltpu.SMEM)
    anywhere = pl.BlockSpec(memory_space=pl.ANY)
    rows = pl.BlockSpec((SHARE, 128), lambda i: (i, 0))
    return pl.pallas_call(
        final_kernel,
        grid=(PLANES,),
        in_specs=[smem] * 3 + [anywhere] * 15 + [rows] * 2,
        out_specs=pl.BlockSpec((1, NB, SHARE), lambda i: (i, 0, 0)),
        out_shape=jax.ShapeDtypeStruct((PLANES, NB, SHARE), jnp.float32),
        scratch_shapes=[
            pltpu.VMEM((KZ, NB, VLANES), jnp.bfloat16),
            pltpu.VMEM((80, 512), jnp.float32),
            pltpu.SemaphoreType.DMA((45,)),
        ],
        compiler_params=pltpu.CompilerParams(vmem_limit_bytes=VMEM_LIMIT),
        cost_estimate=pl.CostEstimate(flops=2_000_000_000, bytes_accessed=9_000_000, transcendentals=0),
        name="contract",
    )(where, off_a, off_b, own, *parts, s_a, s_b)


def local(occupation, q_offsets, coupling, window_bins, lorentz_table, lattice):
    slab = lax.axis_index("ka")
    share = lax.axis_index("pb")
    core = share % 2

    def core_swap(array):
        return lax.ppermute(array, "pb", [(i, i ^ 1) for i in range(16)])

    half = lax.dynamic_slice_in_dim(occupation, core * (PLANES // 2), PLANES // 2, 0)
    steps = [(0, 1), (0, 3), (1, 0), (1, 1), (1, 3), (0, 2), (1, 2)]
    fetched, sources = [], []
    for dy, dx in steps:
        pairs = [(i, ((i // 4) ^ dy) * 4 + (i % 4 + dx) % 4) for i in range(8)]
        fetched.append(lax.ppermute(half, "ka", pairs))
        sources.append(((slab // 4) ^ dy) * 4 + (slab % 4 + 4 - dx) % 4)
    where = jnp.stack([slab, core, share] + sources).astype(jnp.int32)

    small = jnp.zeros((16, NM), jnp.bfloat16)
    small = small.at[:, 0].set(window_bins[0].astype(jnp.bfloat16)).at[:3, 1].set(q_offsets[0].astype(jnp.bfloat16))
    pay = jnp.concatenate(
        [jnp.pad(coupling[0], ((0, 0), (0, RP - NR), (0, 0))).reshape(2 * RP, CH), jnp.pad(small.reshape(1, CH), ((0, 15), (0, 0)))], axis=0
    )
    pair = jnp.concatenate([pay, lax.ppermute(pay, "pb", [(i, i ^ 2) for i in range(16)])], axis=0)
    group = [pair] + [lax.ppermute(pair, "pb", [(i, (i + 4 * d) % 16) for i in range(16)]) for d in (1, 3, 2)]
    other = [core_swap(array) for array in group]

    vectors = jnp.pad(lattice, ((0, 0), (0, RW - NR)))
    kz = slab * PLANES + jnp.arange(PLANES, dtype=jnp.int32)
    kx = share * ROWS + jnp.arange(ROWS, dtype=jnp.int32)
    first = kz[:, None, None] * vectors[2] + kx[None, :, None] * vectors[0]
    second = jnp.arange(KY, dtype=jnp.int32)[:, None] * vectors[1]
    index = jnp.concatenate([first.reshape(PLANES * ROWS, RW), second], axis=0) % KX
    angle = index.astype(jnp.float32) * (2.0 * math.pi / KX)
    cosine, sine = jnp.cos(angle), jnp.sin(angle)
    cut = PLANES * ROWS
    phases = make_phases(
        cosine[:cut].reshape(PLANES, ROWS, RW), sine[:cut].reshape(PLANES, ROWS, RW), cosine[cut:], sine[cut:]
    )

    s_a, off_a = strengths(lorentz_table, group, phases)
    s_b, off_b = strengths(lorentz_table, other, phases)
    swapped = [core_swap(array) for array in fetched]
    return contract(where, off_a, off_b, occupation, fetched + swapped, s_a, s_b)


def solution(mesh):
    in_specs = (
        P("ka", None, None),
        P("pb", None),
        P("pb", None, None, None),
        P("pb", None),
        P(),
        P(),
    )
    out_specs = P("ka", None, "pb")
    return jax.shard_map(local, mesh=mesh, in_specs=in_specs, out_specs=out_specs, check_vma=False)
```

```python
import math

import jax
import jax.numpy as jnp
from jax import lax
from jax.experimental import pallas as pl
from jax.experimental.pallas import tpu as pltpu
from jax.sharding import PartitionSpec as P

KX = 80
KY = 80
KZ = 80
NB = 4
NM = 6
NR = 200
RW = 256
CH = 96
NBIN = 32
QG = 8
PLANES = 10
HP = PLANES // 2
PARTS = 4
WHICH = (0, 1, 3, 5)
ROWS = 5
HALF = KY // 2
SHARE = ROWS * KY
POINTS = PLANES * ROWS * HALF
PAY = 2 * CH + 16
SLOTS = 384
FRONT = 128
BACK = 512
VLANES = FRONT + KX * KY + BACK
WIN = 640
STEP = 400
UNROLL = 5
VMEM_LIMIT = 28 * 1024 * 1024
F32 = jnp.float32
BF16 = jnp.bfloat16


def smem():
    return pl.BlockSpec(memory_space=pltpu.SMEM)


def vmem():
    return pl.BlockSpec(memory_space=pltpu.VMEM)


def anywhere():
    return pl.BlockSpec(memory_space=pl.ANY)


def iota(shape, axis):
    return lax.broadcasted_iota(jnp.int32, shape, axis)


def pack_kernel(off_ref, bins_ref, coupling_ref, pay_ref):
    row = iota((CH, CH), 0)
    moved = jnp.where(iota((CH, CH), 1) == (row & 15) * NM + (row >> 4), 1.0, 0.0).astype(BF16)
    pay_ref[:, NR:] = jnp.zeros((PAY, RW - NR), BF16)
    for part in range(2):
        block = jnp.dot(moved, coupling_ref[part], preferred_element_type=F32)
        pay_ref[part * CH : (part + 1) * CH, :NR] = block.astype(BF16)
    lane = iota((16, 128), 1) & 15
    line = iota((16, 128), 0)
    small = jnp.zeros((16, 128), F32)
    for pair in range(NB * NB):
        small = jnp.where((line == 0) & (lane == pair), bins_ref[0, pair].astype(F32), small)
    for axis in range(3):
        small = jnp.where((line == 1) & (lane == axis), off_ref[0, axis].astype(F32), small)
    pay_ref[2 * CH :, :128] = small.astype(BF16)
    pay_ref[2 * CH :, 128:] = jnp.zeros((16, RW - 128), BF16)


def pack(q_offsets, window_bins, coupling):
    return pl.pallas_call(
        pack_kernel,
        in_specs=[smem(), smem(), vmem()],
        out_specs=vmem(),
        out_shape=jax.ShapeDtypeStruct((PAY, RW), BF16),
        name="pack",
    )(q_offsets, window_bins, coupling)


def sine_of(turns):
    x = turns * (math.pi / 40)
    y = x * x
    s = -2.3889859e-08
    for c in (2.7525562e-06, -1.9840874e-04, 8.3333310e-03, -1.6666667e-01, 1.0):
        s = s * y + c
    return x * s


def cos_sin(steps):
    t = steps - 80.0 * jnp.round(steps * (1.0 / 80.0))
    a = jnp.abs(t)
    cosine = sine_of(20.0 - a)
    folded = jnp.where(a > 20.0, 40.0 - a, a)
    sine = sine_of(jnp.where(t < 0.0, -folded, folded))
    return cosine, sine


def order(lattice):
    lane = iota((8, 256), 1)
    even = jnp.where((jnp.broadcast_to(lattice[1:2, :], (8, 256)) & 1) == 0, 1, 0)
    real = lane < NR
    is_even = jnp.where(real, even, 0).astype(BF16)
    before = jnp.where(iota((256, 256), 0) < iota((256, 256), 1), 1.0, 0.0).astype(BF16)
    rank = jnp.dot(is_even, before, preferred_element_type=F32).astype(jnp.int32)
    count = jnp.sum(is_even[:1].astype(F32), axis=1, keepdims=True).astype(jnp.int32)
    base = jnp.where(count > 128, 256, 128)
    slot = jnp.where(even == 1, rank, lane - rank + base)
    slot = jnp.where(real, slot, -1)[:1]
    count = count[0, 0]
    wide = count > 128
    third = (wide & (count < NR)) | (count < NR - 128)
    place = jnp.where(iota((SLOTS, 256), 0) == slot, 1.0, 0.0).astype(BF16)
    return place, third, wide


def phase_kernel(where_ref, lattice_ref, out_ref, out3_ref):
    lattice = lattice_ref[...]
    place, third, _ = order(lattice)
    vectors = lax.dot_general(lattice.astype(BF16), place, (((1,), (1,)), ((), ())), preferred_element_type=F32)
    n = PLANES * ROWS
    row = iota((56, SLOTS), 0)
    upper = (row * 52) >> 8
    kz = (where_ref[0] * PLANES + upper).astype(F32)
    kx = (where_ref[2] * ROWS + row - ROWS * upper).astype(F32)
    ac, an = cos_sin(kx * vectors[0:1] + kz * vectors[2:3])
    ky = iota((HALF, SLOTS), 0).astype(F32)
    bc, bs = cos_sin(ky * vectors[1:2])

    def tile(t, ref, lane):
        cols = slice(t * 128, (t + 1) * 128)
        c, s = bc[:, cols], bs[:, cols]
        for r in range(0, n, 2):
            cosine, sine = [], []
            for k in (r, r + 1):
                u, v = ac[k : k + 1, cols], an[k : k + 1, cols]
                cosine.append(u * c - v * s)
                sine.append(v * c + u * s)
            rows = slice(r * HALF, (r + 2) * HALF)
            ref[rows, lane : lane + 128] = jnp.concatenate(cosine, axis=0).astype(BF16)
            ref[rows, lane + 128 : lane + 256] = jnp.concatenate(sine, axis=0).astype(BF16)

    tile(0, out_ref, 0)
    tile(1, out_ref, 256)

    @pl.when(third)
    def _():
        tile(2, out3_ref, 0)


def make_phases(where, lattice):
    return pl.pallas_call(
        phase_kernel,
        in_specs=[smem(), vmem()],
        out_specs=[vmem()] * 2,
        out_shape=[jax.ShapeDtypeStruct((POINTS, 512), BF16), jax.ShapeDtypeStruct((POINTS, 256), BF16)],
        compiler_params=pltpu.CompilerParams(vmem_limit_bytes=VMEM_LIMIT),
        cost_estimate=pl.CostEstimate(flops=1_500_000_000, bytes_accessed=3_000_000, transcendentals=0),
        name="phases",
    )(where, lattice)


def strength_kernel(table_ref, lattice_ref, p0, p1, p2, p3, ph_ref, ph3_ref, s_ref, off_ref, mixed_ref, g_ref, w_ref):
    for slot in range(QG):
        ref = (p0, p1, p2, p3)[slot // 2]
        start = (slot % 2) * PAY
        for part in range(2):
            for mode in range(NM):
                source = start + part * CH + mode * 16
                mixed_ref[part, mode * 128 + slot * 16 : mode * 128 + slot * 16 + 16, :] = ref[source : source + 16, :]
        line = ref[start + 2 * CH : start + 2 * CH + 16, :128].astype(F32)[:8]
        small = line if slot == 0 else jnp.where(iota((8, 128), 1) >> 4 == slot, line, small)
    off_ref[...] = small.astype(jnp.int32)
    place, third, wide = order(lattice_ref[...])
    general = third | wide

    def fill(first, count):
        span = count * 128
        rows = place[first * 128 : first * 128 + span]
        both = (((1,), (1,)), ((), ()))
        real = lax.dot_general(rows, mixed_ref[0], both, preferred_element_type=F32)
        imag = lax.dot_general(rows, mixed_ref[1], both, preferred_element_type=F32)
        minus = (-imag).astype(BF16)
        real = real.astype(BF16)
        imag = imag.astype(BF16)
        for t in range(count):
            here = slice(t * 128, (t + 1) * 128)
            low = (first + t) * 256
            for mode in range(NM):
                lanes = slice(mode * 128, (mode + 1) * 128)
                left = slice(mode * 256, mode * 256 + 128)
                right = slice(mode * 256 + 128, mode * 256 + 256)
                g_ref[low : low + 128, left] = real[here, lanes]
                g_ref[low : low + 128, right] = imag[here, lanes]
                g_ref[low + 128 : low + 256, left] = minus[here, lanes]
                g_ref[low + 128 : low + 256, right] = real[here, lanes]

    fill(0, 2)
    pl.when(third)(lambda: fill(2, 1))
    level = jnp.where(iota((NBIN, 128), 0) == small[:1].astype(jnp.int32), 1.0, 0.0).astype(BF16)
    table = table_ref[...]
    weights = None
    for _ in range(3):
        piece = table.astype(BF16)
        table = table - piece.astype(F32)
        got = jnp.dot(piece, level, preferred_element_type=F32)
        weights = got if weights is None else weights + got
    w_ref[:NM, :] = weights

    def square(x):
        return x[:, :128] * x[:, :128] + x[:, 128:] * x[:, 128:]

    def run(full):
        sign = jnp.where(wide, 1.0, -1.0)

        def body(step, carry):
            rows = pl.ds(pl.multiple_of(step * STEP, STEP), STEP)
            plus = minus = None
            for mode in range(NM):
                cols = slice(mode * 256, (mode + 1) * 256)
                one = jnp.dot(ph_ref[rows, :256], g_ref[:256, cols], preferred_element_type=F32)
                two = jnp.dot(ph_ref[rows, 256:], g_ref[256:512, cols], preferred_element_type=F32)
                if full:
                    three = jnp.dot(ph3_ref[rows, :], g_ref[512:, cols], preferred_element_type=F32)
                    three = jnp.where(third, three, 0.0)
                    sums, differences = one + two + three, one + sign * two - three
                else:
                    sums, differences = one + two, one - two
                weight = w_ref[mode : mode + 1, :]
                up, down = square(sums) * weight, square(differences) * weight
                plus = up if plus is None else plus + up
                minus = down if minus is None else minus + down
            s_ref[0, rows, :] = plus
            s_ref[1, rows, :] = minus
            return carry

        lax.fori_loop(0, POINTS // STEP, body, 0)

    pl.when(jnp.logical_not(general))(lambda: run(False))
    pl.when(general)(lambda: run(True))


def strengths(table, lattice, pays, phases, phases3):
    return pl.pallas_call(
        strength_kernel,
        in_specs=[vmem()] * 8,
        out_specs=[vmem()] * 2,
        out_shape=[jax.ShapeDtypeStruct((2, POINTS, 128), F32), jax.ShapeDtypeStruct((8, 128), jnp.int32)],
        scratch_shapes=[
            pltpu.VMEM((2, NM * 128, RW), BF16),
            pltpu.VMEM((768, 2 * NM * 128), BF16),
            pltpu.VMEM((8, 128), F32),
        ],
        compiler_params=pltpu.CompilerParams(vmem_limit_bytes=VMEM_LIMIT),
        cost_estimate=pl.CostEstimate(flops=4_000_000_000, bytes_accessed=6_000_000, transcendentals=0),
        name="strengths",
    )(table, lattice, *pays, phases, phases3)


def final_kernel(where_ref, off_a_ref, off_b_ref, own, *refs):
    parts = refs[: 2 * PARTS]
    sa_ref, sb_ref, out_ref, v_ref, arr_ref, off_ref, sem = refs[2 * PARTS :]
    slab = where_ref[0]
    core = where_ref[1]
    share = where_ref[2]
    copies = [
        pltpu.make_async_copy(off_a_ref, off_ref.at[0], sem.at[0]),
        pltpu.make_async_copy(off_b_ref, off_ref.at[1], sem.at[1]),
    ]

    def bring(src, plane, count):
        dst = v_ref.at[pl.ds(plane, count)]
        copies.append(pltpu.make_async_copy(src, dst.at[:, :, FRONT : FRONT + KX * KY], sem.at[len(copies)]))
        copies.append(pltpu.make_async_copy(src.at[:, :, :BACK], dst.at[:, :, FRONT + KX * KY :], sem.at[len(copies)]))
        copies.append(pltpu.make_async_copy(src.at[:, :, KX * KY - FRONT :], dst.at[:, :, :FRONT], sem.at[len(copies)]))

    bring(own, slab * PLANES, PLANES)
    for index in range(PARTS):
        for which in range(parts[index].shape[0]):
            source = where_ref[3 + WHICH[index] + which]
            bring(parts[index].at[which], source * PLANES + core * HP, HP)
            bring(parts[PARTS + index].at[which], source * PLANES + (1 - core) * HP, HP)
    for copy in copies:
        copy.start()

    ky = lax.rem(iota((NB, 512), 1), KY)
    row = iota((80, 256), 0)
    col = iota((80, 256), 1)
    gain = (row < 64) & (row >> 2 == col >> 4) & (row & 3 == col & 3)
    loss = (row >= 64) & (row - 64 == (col >> 2) & 3)
    spread = (jnp.where(gain, 1.0, 0.0) - jnp.where(loss, 1.0, 0.0)).astype(BF16)
    pick = jnp.where((iota((8, 128), 1) >> 2) & 3 == iota((8, 128), 0), 1.0, 0.0).astype(BF16)
    home = pl.multiple_of(((share * SHARE + FRONT) >> 7) * 128, 128)
    turn = lax.rem(WIN - lax.rem(share * SHARE, 128), WIN)
    arr_ref[:, 64:80, :] = jnp.zeros((UNROLL, 16, 512), F32)
    for copy in copies:
        copy.wait()

    def shift(step, lane):
        for slot in range(2 * QG):
            base = (slot % QG) * 16
            qx = off_ref[slot // QG, 1, base]
            qy = off_ref[slot // QG, 1, base + 1]
            qz = off_ref[slot // QG, 1, base + 2]
            plane = lax.rem(slab * PLANES + step + qz, KZ)
            first = lax.rem(share * ROWS + qx, KX) * KY
            start = first + qy + (FRONT - KY)
            aligned = pl.multiple_of((start >> 7) * 128, 128)
            window = v_ref[plane, :, pl.ds(aligned, WIN)].astype(F32)
            late = pltpu.roll(window, lax.rem(WIN - (start - aligned), WIN), 1)
            early = pltpu.roll(late, WIN - KY, 1)
            arr_ref[lane, NB * slot : NB * (slot + 1), :] = jnp.where(ky + qy < KY, early[:, :512], late[:, :512])
        window = v_ref[slab * PLANES + step, :, pl.ds(home, WIN)].astype(F32)
        arr_ref[lane, 64:68, :] = pltpu.roll(window, turn, 1)[:, :512]

    def combine(step, lane):
        arrived = arr_ref[lane].astype(BF16)
        diff = lax.dot_general(arrived, spread, (((0,), (0,)), ((), ())), preferred_element_type=F32)
        terms = []
        for kx in range(ROWS):
            for upper in range(2):
                rows = pl.ds(pl.multiple_of((step * ROWS + kx) * HALF, HALF), HALF)
                here = slice((2 * kx + upper) * HALF, (2 * kx + upper + 1) * HALF)
                terms.append(sa_ref[upper, rows, :] * diff[here, :128] + sb_ref[upper, rows, :] * diff[here, 128:])
        term = jnp.concatenate(terms, axis=0)
        result = None
        for _ in range(3):
            piece = term.astype(BF16)
            term = term - piece.astype(F32)
            got = lax.dot_general(pick, piece, (((1,), (1,)), ((), ())), preferred_element_type=F32)
            result = got if result is None else result + got
        out_ref[step] = result[:NB] * (1.0 / (2 * QG * NM))

    def body(step, carry):
        for lane in range(UNROLL):
            shift(step * UNROLL + lane, lane)
        for lane in range(UNROLL):
            combine(step * UNROLL + lane, lane)
        return carry

    lax.fori_loop(0, PLANES // UNROLL, body, 0)


def contract(where, off_a, off_b, own, parts, s_a, s_b):
    return pl.pallas_call(
        final_kernel,
        in_specs=[smem()] + [anywhere()] * (3 + 2 * PARTS) + [vmem()] * 2,
        out_specs=vmem(),
        out_shape=jax.ShapeDtypeStruct((PLANES, NB, SHARE), F32),
        scratch_shapes=[
            pltpu.VMEM((KZ, NB, VLANES), BF16),
            pltpu.VMEM((UNROLL, 80, 512), F32),
            pltpu.SMEM((2, 8, 128), jnp.int32),
            pltpu.SemaphoreType.DMA((47,)),
        ],
        compiler_params=pltpu.CompilerParams(vmem_limit_bytes=VMEM_LIMIT),
        cost_estimate=pl.CostEstimate(flops=2_000_000_000, bytes_accessed=9_000_000, transcendentals=0),
        name="contract",
    )(where, off_a, off_b, own, *parts, s_a, s_b)


def local(occupation, q_offsets, coupling, window_bins, lorentz_table, lattice):
    slab = lax.axis_index("ka")
    share = lax.axis_index("pb")
    core = share % 2
    vectors = jnp.pad(lattice, ((0, 5), (0, RW - NR)))

    def place(ylo, x, z, yhi, c):
        return ((ylo * 4 + x) * 16) + z * 4 + yhi * 2 + c

    def move(array, to):
        grid = [(yl, x, z, yh, c) for yl in range(2) for x in range(4) for z in range(4) for yh in range(2) for c in range(2)]
        return lax.ppermute(array, ("ka", "pb"), [(place(*at), place(*to(*at))) for at in grid])

    def core_swap(array):
        return move(array, lambda yl, x, z, yh, c: (yl, x, z, yh, 1 - c))

    pay = pack(q_offsets, window_bins, jnp.swapaxes(coupling[0], 1, 2))
    pair = jnp.concatenate([pay, move(pay, lambda yl, x, z, yh, c: (1 - yl, x, z, 1 - yh, c))], axis=0)
    group = [pair] + [move(pair, lambda yl, x, z, yh, c: (yl, x, (z + d) % 4, yh, c)) for d in (1, 3, 2)]
    other = [core_swap(array) for array in group]
    half = lax.dynamic_slice_in_dim(occupation, core * HP, HP, 0)[None]
    beyond = move(half, lambda yl, x, z, yh, c: (1 - yl, x, z, yh, c))
    both = jnp.concatenate([half, beyond], axis=0)
    fetched = [beyond] + [move(both, lambda yl, x, z, yh, c: (yl, (x + d) % 4, z, yh, c)) for d in (1, 3, 2)]
    swapped = [core_swap(array) for array in fetched]
    ylo, x = slab // 4, slab % 4
    sources = [(1 - ylo) * 4 + x]
    for d in (1, 3, 2):
        sources += [ylo * 4 + (x + 4 - d) % 4, (1 - ylo) * 4 + (x + 4 - d) % 4]
    where = jnp.stack([slab, core, share] + sources).astype(jnp.int32)

    phases, phases3 = make_phases(where, vectors)
    table = lorentz_table.T
    s_a, off_a = strengths(table, vectors, group, phases, phases3)
    s_b, off_b = strengths(table, vectors, other, phases, phases3)
    return contract(where, off_a, off_b, occupation, fetched + swapped, s_a, s_b)


def solution(mesh):
    in_specs = (
        P("ka", None, None),
        P("pb", None),
        P("pb", None, None, None),
        P("pb", None),
        P(),
        P(),
    )
    out_specs = P("ka", None, "pb")
    return jax.shard_map(local, mesh=mesh, in_specs=in_specs, out_specs=out_specs, check_vma=False)
```

```python
import math

import jax
import jax.numpy as jnp
from jax import lax
from jax.experimental import pallas as pl
from jax.experimental.pallas import tpu as pltpu
from jax.sharding import PartitionSpec as P

KX = 80
KY = 80
KZ = 80
NB = 4
NM = 6
NR = 200
RW = 256
CH = 96
NBIN = 32
QG = 8
PLANES = 10
HP = PLANES // 2
PARTS = 5
WHICH = (0, 1, 2, 3, 5)
ROWS = 5
HALF = KY // 2
SHARE = ROWS * KY
POINTS = PLANES * ROWS * HALF
PAY = 2 * CH + 16
SLOTS = 384
FRONT = 128
BACK = 512
VLANES = FRONT + KX * KY + BACK
WIN = 640
STEP = 400
UNROLL = 10
VMEM_LIMIT = 28 * 1024 * 1024
F32 = jnp.float32
BF16 = jnp.bfloat16


def smem():
    return pl.BlockSpec(memory_space=pltpu.SMEM)


def vmem():
    return pl.BlockSpec(memory_space=pltpu.VMEM)


def anywhere():
    return pl.BlockSpec(memory_space=pl.ANY)


def wrap(value, size):
    return jnp.where(value >= size, value - size, value)


def iota(shape, axis):
    return lax.broadcasted_iota(jnp.int32, shape, axis)


def pack_kernel(off_ref, bins_ref, coupling_ref, pay_ref):
    row = iota((CH, CH), 0)
    moved = jnp.where(iota((CH, CH), 1) == (row & 15) * NM + (row >> 4), 1.0, 0.0).astype(BF16)
    pay_ref[:, NR:] = jnp.zeros((PAY, RW - NR), BF16)
    for part in range(2):
        block = jnp.dot(moved, coupling_ref[part], preferred_element_type=F32)
        pay_ref[part * CH : (part + 1) * CH, :NR] = block.astype(BF16)
    lane = iota((16, 128), 1) & 15
    line = iota((16, 128), 0)
    small = jnp.zeros((16, 128), F32)
    for pair in range(NB * NB):
        small = jnp.where((line == 0) & (lane == pair), bins_ref[0, pair].astype(F32), small)
    for axis in range(3):
        small = jnp.where((line == 1) & (lane == axis), off_ref[0, axis].astype(F32), small)
    pay_ref[2 * CH :, :128] = small.astype(BF16)
    pay_ref[2 * CH :, 128:] = jnp.zeros((16, RW - 128), BF16)


def pack(q_offsets, window_bins, coupling):
    return pl.pallas_call(
        pack_kernel,
        in_specs=[smem(), smem(), vmem()],
        out_specs=vmem(),
        out_shape=jax.ShapeDtypeStruct((PAY, RW), BF16),
        name="pack",
    )(q_offsets, window_bins, coupling)


def sine_of(turns):
    x = turns * (math.pi / 40)
    y = x * x
    s = -2.3889859e-08
    for c in (2.7525562e-06, -1.9840874e-04, 8.3333310e-03, -1.6666667e-01, 1.0):
        s = s * y + c
    return x * s


def cos_sin(steps):
    t = steps - 80.0 * jnp.round(steps * (1.0 / 80.0))
    a = jnp.abs(t)
    cosine = sine_of(20.0 - a)
    folded = jnp.where(a > 20.0, 40.0 - a, a)
    sine = sine_of(jnp.where(t < 0.0, -folded, folded))
    return cosine, sine


def order(lattice):
    lane = iota((8, 256), 1)
    even = jnp.where((jnp.broadcast_to(lattice[1:2, :], (8, 256)) & 1) == 0, 1, 0)
    real = lane < NR
    is_even = jnp.where(real, even, 0).astype(BF16)
    before = jnp.where(iota((256, 256), 0) < iota((256, 256), 1), 1.0, 0.0).astype(BF16)
    rank = jnp.dot(is_even, before, preferred_element_type=F32).astype(jnp.int32)
    count = jnp.sum(is_even[:1].astype(F32), axis=1, keepdims=True).astype(jnp.int32)
    base = jnp.where(count > 128, 256, 128)
    slot = jnp.where(even == 1, rank, lane - rank + base)
    slot = jnp.where(real, slot, -1)[:1]
    count = count[0, 0]
    wide = count > 128
    third = (wide & (count < NR)) | (count < NR - 128)
    place = jnp.where(iota((SLOTS, 256), 0) == slot, 1.0, 0.0).astype(BF16)
    return place, third, wide


def widen(lattice_ref, wide_ref):
    wide_ref[...] = jnp.zeros((8, RW), jnp.int32)
    wide_ref[:3, :NR] = lattice_ref[...]
    return wide_ref[...]


def phase_kernel(where_ref, lattice_ref, out_ref, out3_ref, wide_ref):
    lattice = widen(lattice_ref, wide_ref)
    place, third, _ = order(lattice)
    vectors = lax.dot_general(lattice.astype(BF16), place, (((1,), (1,)), ((), ())), preferred_element_type=F32)
    n = PLANES * ROWS
    row = iota((56, SLOTS), 0)
    upper = (row * 52) >> 8
    kz = (where_ref[0] * PLANES + upper).astype(F32)
    kx = (where_ref[2] * ROWS + row - ROWS * upper).astype(F32)
    ac, an = cos_sin(kx * vectors[0:1] + kz * vectors[2:3])
    ky = iota((HALF, SLOTS), 0).astype(F32)
    bc, bs = cos_sin(ky * vectors[1:2])

    def tile(t, ref, lane):
        cols = slice(t * 128, (t + 1) * 128)
        c, s = bc[:, cols], bs[:, cols]
        for r in range(0, n, 2):
            cosine, sine = [], []
            for k in (r, r + 1):
                u, v = ac[k : k + 1, cols], an[k : k + 1, cols]
                cosine.append(u * c - v * s)
                sine.append(v * c + u * s)
            rows = slice(r * HALF, (r + 2) * HALF)
            ref[rows, lane : lane + 128] = jnp.concatenate(cosine, axis=0).astype(BF16)
            ref[rows, lane + 128 : lane + 256] = jnp.concatenate(sine, axis=0).astype(BF16)

    tile(0, out_ref, 0)
    tile(1, out_ref, 256)

    @pl.when(third)
    def _():
        tile(2, out3_ref, 0)


def make_phases(where, lattice):
    return pl.pallas_call(
        phase_kernel,
        in_specs=[smem(), vmem()],
        out_specs=[vmem()] * 2,
        out_shape=[jax.ShapeDtypeStruct((POINTS, 512), BF16), jax.ShapeDtypeStruct((POINTS, 256), BF16)],
        scratch_shapes=[pltpu.VMEM((8, RW), jnp.int32)],
        compiler_params=pltpu.CompilerParams(vmem_limit_bytes=VMEM_LIMIT),
        cost_estimate=pl.CostEstimate(flops=1_500_000_000, bytes_accessed=3_000_000, transcendentals=0),
        name="phases",
    )(where, lattice)


def strength_kernel(table_ref, lattice_ref, *refs):
    pays = refs[:8]
    ph_ref, ph3_ref, s_ref, off_ref, mixed_ref, g_ref, w_ref, wide_ref = refs[8:]
    for slot in range(2 * QG):
        ref = pays[slot // 2]
        start = (slot % 2) * PAY
        group, inner = slot // QG, slot % QG
        for part in range(2):
            for mode in range(NM):
                source = start + part * CH + mode * 16
                mixed_ref[group, part, mode * 128 + inner * 16 : mode * 128 + inner * 16 + 16, :] = ref[source : source + 16, :]
        line = ref[start + 2 * CH : start + 2 * CH + 16, :128].astype(F32)[:8]
        small = line if inner == 0 else jnp.where(iota((8, 128), 1) >> 4 == inner, line, small)
        if inner == QG - 1:
            off_ref[group] = small.astype(jnp.int32)
            level = jnp.where(iota((NBIN, 128), 0) == small[:1].astype(jnp.int32), 1.0, 0.0).astype(BF16)
            table = table_ref[...]
            weights = None
            for _ in range(3):
                piece = table.astype(BF16)
                table = table - piece.astype(F32)
                got = jnp.dot(piece, level, preferred_element_type=F32)
                weights = got if weights is None else weights + got
            w_ref[group, :NM, :] = weights
    place, third, wide = order(widen(lattice_ref, wide_ref))
    general = third | wide

    def fill(first, count):
        span = count * 128
        rows = place[first * 128 : first * 128 + span]
        both = (((1,), (1,)), ((), ()))
        for group in range(2):
            real = lax.dot_general(rows, mixed_ref[group, 0], both, preferred_element_type=F32)
            imag = lax.dot_general(rows, mixed_ref[group, 1], both, preferred_element_type=F32)
            minus = (-imag).astype(BF16)
            real = real.astype(BF16)
            imag = imag.astype(BF16)
            for t in range(count):
                here = slice(t * 128, (t + 1) * 128)
                low = (first + t) * 256
                for mode in range(NM):
                    lanes = slice(mode * 128, (mode + 1) * 128)
                    left = slice(mode * 256, mode * 256 + 128)
                    right = slice(mode * 256 + 128, mode * 256 + 256)
                    g_ref[group, low : low + 128, left] = real[here, lanes]
                    g_ref[group, low : low + 128, right] = imag[here, lanes]
                    g_ref[group, low + 128 : low + 256, left] = minus[here, lanes]
                    g_ref[group, low + 128 : low + 256, right] = real[here, lanes]

    fill(0, 2)
    pl.when(third)(lambda: fill(2, 1))

    def square(x):
        return x[:, :128] * x[:, :128] + x[:, 128:] * x[:, 128:]

    def run(full):
        sign = jnp.where(wide, 1.0, -1.0)

        def body(step, carry):
            rows = pl.ds(pl.multiple_of(step * STEP, STEP), STEP)
            for group in range(2):
                plus = minus = None
                for mode in range(NM):
                    cols = slice(mode * 256, (mode + 1) * 256)
                    one = jnp.dot(ph_ref[rows, :256], g_ref[group, :256, cols], preferred_element_type=F32)
                    two = jnp.dot(ph_ref[rows, 256:], g_ref[group, 256:512, cols], preferred_element_type=F32)
                    if full:
                        three = jnp.dot(ph3_ref[rows, :], g_ref[group, 512:, cols], preferred_element_type=F32)
                        three = jnp.where(third, three, 0.0)
                        sums, differences = one + two + three, one + sign * two - three
                    else:
                        sums, differences = one + two, one - two
                    weight = w_ref[group, mode : mode + 1, :]
                    up, down = square(sums) * weight, square(differences) * weight
                    plus = up if plus is None else plus + up
                    minus = down if minus is None else minus + down
                s_ref[0, rows, group * 128 : (group + 1) * 128] = plus
                s_ref[1, rows, group * 128 : (group + 1) * 128] = minus
            return carry

        lax.fori_loop(0, POINTS // STEP, body, 0)

    pl.when(jnp.logical_not(general))(lambda: run(False))
    pl.when(general)(lambda: run(True))


def strengths(table, lattice, pays, phases, phases3):
    return pl.pallas_call(
        strength_kernel,
        in_specs=[vmem()] * 12,
        out_specs=[vmem()] * 2,
        out_shape=[jax.ShapeDtypeStruct((2, POINTS, 256), F32), jax.ShapeDtypeStruct((2, 8, 128), jnp.int32)],
        scratch_shapes=[
            pltpu.VMEM((2, 2, NM * 128, RW), BF16),
            pltpu.VMEM((2, 768, 2 * NM * 128), BF16),
            pltpu.VMEM((2, 8, 128), F32),
            pltpu.VMEM((8, RW), jnp.int32),
        ],
        compiler_params=pltpu.CompilerParams(vmem_limit_bytes=VMEM_LIMIT),
        cost_estimate=pl.CostEstimate(flops=1_000_000_000, bytes_accessed=1000, transcendentals=0),
        name="strengths",
    )(table, lattice, *pays, phases, phases3)


def final_kernel(where_ref, offsets_ref, own, *refs):
    parts = refs[: 2 * PARTS]
    s_ref, out_ref, v_ref, arr_ref, off_ref, sem = refs[2 * PARTS :]
    slab = where_ref[0]
    core = where_ref[1]
    share = where_ref[2]
    copies = [
        pltpu.make_async_copy(offsets_ref, off_ref, sem.at[0]),
    ]

    def bring(src, plane, count):
        dst = v_ref.at[pl.ds(plane, count)]
        copies.append(pltpu.make_async_copy(src, dst.at[:, :, FRONT : FRONT + KX * KY], sem.at[len(copies)]))
        copies.append(pltpu.make_async_copy(src.at[:, :, :BACK], dst.at[:, :, FRONT + KX * KY :], sem.at[len(copies)]))
        copies.append(pltpu.make_async_copy(src.at[:, :, KX * KY - FRONT :], dst.at[:, :, :FRONT], sem.at[len(copies)]))

    bring(own, slab * PLANES, PLANES)
    for index in range(PARTS):
        for which in range(parts[index].shape[0]):
            source = where_ref[3 + WHICH[index] + which]
            bring(parts[index].at[which], source * PLANES + core * HP, HP)
            bring(parts[PARTS + index].at[which], source * PLANES + (1 - core) * HP, HP)
    for copy in copies:
        copy.start()

    ky = lax.rem(iota((NB, 512), 1), KY)
    row = iota((80, 256), 0)
    col = iota((80, 256), 1)
    gain = (row < 64) & (row >> 2 == col >> 4) & (row & 3 == col & 3)
    loss = (row >= 64) & (row - 64 == (col >> 2) & 3)
    spread = (jnp.where(gain, 1.0, 0.0) - jnp.where(loss, 1.0, 0.0)).astype(BF16)
    pick = jnp.where((iota((8, 128), 1) >> 2) & 3 == iota((8, 128), 0), 1.0, 0.0).astype(BF16)
    home = pl.multiple_of(((share * SHARE + FRONT) >> 7) * 128, 128)
    turn = lax.rem(WIN - lax.rem(share * SHARE, 128), WIN)
    arr_ref[:, 64:80, :] = jnp.zeros((UNROLL, 16, 512), F32)
    for copy in copies:
        copy.wait()

    def shift(step, lane):
        for slot in range(2 * QG):
            base = (slot % QG) * 16
            qx = off_ref[slot // QG, 1, base]
            qy = off_ref[slot // QG, 1, base + 1]
            qz = off_ref[slot // QG, 1, base + 2]
            plane = wrap(slab * PLANES + step + qz, KZ)
            first = wrap(share * ROWS + qx, KX) * KY
            start = first + qy + (FRONT - KY)
            aligned = pl.multiple_of((start >> 7) * 128, 128)
            window = v_ref[plane, :, pl.ds(aligned, WIN)].astype(F32)
            late = pltpu.roll(window, wrap(WIN - (start - aligned), WIN), 1)
            early = pltpu.roll(late, WIN - KY, 1)
            arr_ref[lane, NB * slot : NB * (slot + 1), :] = jnp.where(ky + qy < KY, early[:, :512], late[:, :512])
        window = v_ref[slab * PLANES + step, :, pl.ds(home, WIN)].astype(F32)
        arr_ref[lane, 64:68, :] = pltpu.roll(window, turn, 1)[:, :512]

    def combine(step, lane):
        arrived = arr_ref[lane].astype(BF16)
        diff = lax.dot_general(arrived, spread, (((0,), (0,)), ((), ())), preferred_element_type=F32)
        terms = []
        for kx in range(ROWS):
            for upper in range(2):
                rows = pl.ds(pl.multiple_of((step * ROWS + kx) * HALF, HALF), HALF)
                here = slice((2 * kx + upper) * HALF, (2 * kx + upper + 1) * HALF)
                product = s_ref[upper, rows, :] * diff[here]
                terms.append(product[:, :128] + product[:, 128:])
        term = jnp.concatenate(terms, axis=0)
        result = None
        for _ in range(3):
            piece = term.astype(BF16)
            term = term - piece.astype(F32)
            got = lax.dot_general(pick, piece, (((1,), (1,)), ((), ())), preferred_element_type=F32)
            result = got if result is None else result + got
        out_ref[step] = result[:NB] * (1.0 / (2 * QG * NM))

    def body(step, carry):
        for lane in range(UNROLL):
            shift(step * UNROLL + lane, lane)
        for lane in range(UNROLL):
            combine(step * UNROLL + lane, lane)
        return carry

    lax.fori_loop(0, PLANES // UNROLL, body, 0)


def contract(where, offsets, own, parts, strength):
    return pl.pallas_call(
        final_kernel,
        in_specs=[smem()] + [anywhere()] * (2 + 2 * PARTS) + [vmem()],
        out_specs=vmem(),
        out_shape=jax.ShapeDtypeStruct((PLANES, NB, SHARE), F32),
        scratch_shapes=[
            pltpu.VMEM((KZ, NB, VLANES), BF16),
            pltpu.VMEM((UNROLL, 80, 512), F32),
            pltpu.SMEM((2, 8, 128), jnp.int32),
            pltpu.SemaphoreType.DMA((47,)),
        ],
        compiler_params=pltpu.CompilerParams(vmem_limit_bytes=VMEM_LIMIT),
        cost_estimate=pl.CostEstimate(flops=2_000_000_000, bytes_accessed=9_000_000, transcendentals=0),
        name="contract",
    )(where, offsets, own, *parts, strength)


def local(occupation, q_offsets, coupling, window_bins, lorentz_table, lattice):
    slab = lax.axis_index("ka")
    share = lax.axis_index("pb")
    core = share % 2

    def place(ylo, x, z, yhi, c):
        return ((ylo * 4 + x) * 16) + z * 4 + yhi * 2 + c

    def move(array, to):
        grid = [(yl, x, z, yh, c) for yl in range(2) for x in range(4) for z in range(4) for yh in range(2) for c in range(2)]
        return lax.ppermute(array, ("ka", "pb"), [(place(*at), place(*to(*at))) for at in grid])

    def core_swap(array):
        return move(array, lambda yl, x, z, yh, c: (yl, x, z, yh, 1 - c))

    pay = pack(q_offsets, window_bins, jnp.swapaxes(coupling[0], 1, 2))
    half, pay = lax.optimization_barrier((lax.dynamic_slice_in_dim(occupation, core * HP, HP, 0)[None], pay))
    along = [move(half, lambda yl, x, z, yh, c: (yl, (x + d) % 4, z, yh, c)) for d in (1, 3, 2)]
    twin = move(pay, lambda yl, x, z, yh, c: (1 - yl, x, z, 1 - yh, c))
    ylo, x = slab // 4, slab % 4
    lines = [(ylo, 1), (ylo, 3), (ylo, 2), (1 - ylo, 0), (1 - ylo, 1), (1 - ylo, 3), (1 - ylo, 2)]
    sources = [y * 4 + (x + 4 - d) % 4 for y, d in lines]
    where = jnp.stack([slab, core, share] + sources).astype(jnp.int32)
    pair = jnp.concatenate([pay, twin], axis=0)
    pair, where = lax.optimization_barrier((pair, where))
    phases, phases3 = make_phases(where, lattice)
    group = [pair] + [move(pair, lambda yl, x, z, yh, c: (yl, x, (z + d) % 4, yh, c)) for d in (1, 3, 2)]
    other = [core_swap(array) for array in group]
    near_in = jnp.concatenate([half, along[0]], axis=0)
    far_in = jnp.concatenate(along[1:], axis=0)
    near_in, far_in, phases = lax.optimization_barrier((near_in, far_in, phases))
    near = move(near_in, lambda yl, x, z, yh, c: (1 - yl, x, z, yh, c))
    far = move(far_in, lambda yl, x, z, yh, c: (1 - yl, x, z, 1 - yh, c))
    table = lorentz_table.T
    strength, offsets = strengths(table, lattice, group + other, phases, phases3)
    near, far, strength = lax.optimization_barrier((near, far, strength))
    fetched = along + [near, far]
    swapped = [core_swap(array) for array in fetched]
    return contract(where, offsets, occupation, fetched + swapped, strength)


def solution(mesh):
    in_specs = (
        P("ka", None, None),
        P("pb", None),
        P("pb", None, None, None),
        P("pb", None),
        P(),
        P(),
    )
    out_specs = P("ka", None, "pb")
    return jax.shard_map(local, mesh=mesh, in_specs=in_specs, out_specs=out_specs, check_vma=False)
```

```python
import functools
import math

import jax
import jax.numpy as jnp
from jax import lax
from jax.experimental import pallas as pl
from jax.experimental.pallas import tpu as pltpu
from jax.sharding import PartitionSpec as P

KX = 80
KY = 80
KZ = 80
NB = 4
NM = 6
NR = 200
RW = 256
CH = 96
NBIN = 32
QG = 8
PLANES = 10
HP = PLANES // 2
PARTS = 5
WHICH = (0, 1, 2, 4, 6)
ROWS = 5
HALF = KY // 2
SHARE = ROWS * KY
POINTS = PLANES * ROWS * HALF
PAY = 2 * CH + 16
SLOTS = 384
FRONT = 128
BACK = 512
VLANES = FRONT + KX * KY + BACK
WIN = 640
STEP = 1000
UNROLL = 10
VMEM_LIMIT = 28 * 1024 * 1024
F32 = jnp.float32
BF16 = jnp.bfloat16


def smem():
    return pl.BlockSpec(memory_space=pltpu.SMEM)


def vmem():
    return pl.BlockSpec(memory_space=pltpu.VMEM)


def anywhere():
    return pl.BlockSpec(memory_space=pl.ANY)


def wrap(value, size):
    return jnp.where(value >= size, value - size, value)


def iota(shape, axis):
    return lax.broadcasted_iota(jnp.int32, shape, axis)


def pack_kernel(off_ref, bins_ref, coupling_ref, pay_ref):
    row = iota((CH, CH), 0)
    moved = jnp.where(iota((CH, CH), 1) == (row & 15) * NM + (row >> 4), 1.0, 0.0).astype(BF16)
    pay_ref[:, NR:] = jnp.zeros((PAY, RW - NR), BF16)
    for part in range(2):
        block = jnp.dot(moved, coupling_ref[part], preferred_element_type=F32)
        pay_ref[part * CH : (part + 1) * CH, :NR] = block.astype(BF16)
    lane = iota((16, 128), 1) & 15
    line = iota((16, 128), 0)
    small = jnp.zeros((16, 128), F32)
    for pair in range(NB * NB):
        small = jnp.where((line == 0) & (lane == pair), bins_ref[0, pair].astype(F32), small)
    for axis in range(3):
        small = jnp.where((line == 1) & (lane == axis), off_ref[0, axis].astype(F32), small)
    pay_ref[2 * CH :, :128] = small.astype(BF16)
    pay_ref[2 * CH :, 128:] = jnp.zeros((16, RW - 128), BF16)


def pack(q_offsets, window_bins, coupling):
    return pl.pallas_call(
        pack_kernel,
        in_specs=[smem(), smem(), vmem()],
        out_specs=vmem(),
        out_shape=jax.ShapeDtypeStruct((PAY, RW), BF16),
        name="pack",
    )(q_offsets, window_bins, coupling)


def sine_of(turns):
    x = turns * (math.pi / 40)
    y = x * x
    s = -2.3889859e-08
    for c in (2.7525562e-06, -1.9840874e-04, 8.3333310e-03, -1.6666667e-01, 1.0):
        s = s * y + c
    return x * s


def cos_sin(steps):
    t = steps - 80.0 * jnp.round(steps * (1.0 / 80.0))
    a = jnp.abs(t)
    cosine = sine_of(20.0 - a)
    folded = jnp.where(a > 20.0, 40.0 - a, a)
    sine = sine_of(jnp.where(t < 0.0, -folded, folded))
    return cosine, sine


def order(lattice):
    lane = iota((8, 256), 1)
    even = jnp.where((jnp.broadcast_to(lattice[1:2, :], (8, 256)) & 1) == 0, 1, 0)
    real = lane < NR
    is_even = jnp.where(real, even, 0).astype(BF16)
    before = jnp.where(iota((256, 256), 0) < iota((256, 256), 1), 1.0, 0.0).astype(BF16)
    rank = jnp.dot(is_even, before, preferred_element_type=F32).astype(jnp.int32)
    count = jnp.sum(is_even[:1].astype(F32), axis=1, keepdims=True).astype(jnp.int32)
    base = jnp.where(count > 128, 256, 128)
    slot = jnp.where(even == 1, rank, lane - rank + base)
    slot = jnp.where(real, slot, -1)[:1]
    count = count[0, 0]
    wide = count > 128
    third = (wide & (count < NR)) | (count < NR - 128)
    place = jnp.where(iota((SLOTS, 256), 0) == slot, 1.0, 0.0).astype(BF16)
    return place, third, wide


def widen(lattice_ref, wide_ref):
    wide_ref[...] = jnp.zeros((8, RW), jnp.int32)
    wide_ref[:3, :NR] = lattice_ref[...]
    return wide_ref[...]


def phase_kernel(where_ref, lattice_ref, out_ref, out3_ref, wide_ref):
    lattice = widen(lattice_ref, wide_ref)
    place, third, _ = order(lattice)
    vectors = lax.dot_general(lattice.astype(BF16), place, (((1,), (1,)), ((), ())), preferred_element_type=F32)
    n = PLANES * ROWS
    row = iota((56, SLOTS), 0)
    upper = (row * 52) >> 8
    kz = (where_ref[0] * PLANES + upper).astype(F32)
    kx = (where_ref[2] * ROWS + row - ROWS * upper).astype(F32)
    ac, an = cos_sin(kx * vectors[0:1] + kz * vectors[2:3])
    ky = iota((HALF, SLOTS), 0).astype(F32)
    bc, bs = cos_sin(ky * vectors[1:2])

    def tile(t, ref, lane):
        cols = slice(t * 128, (t + 1) * 128)
        c, s = bc[:, cols], bs[:, cols]
        for r in range(0, n, 2):
            cosine, sine = [], []
            for k in (r, r + 1):
                u, v = ac[k : k + 1, cols], an[k : k + 1, cols]
                cosine.append(u * c - v * s)
                sine.append(v * c + u * s)
            rows = slice(r * HALF, (r + 2) * HALF)
            ref[rows, lane : lane + 128] = jnp.concatenate(cosine, axis=0).astype(BF16)
            ref[rows, lane + 128 : lane + 256] = jnp.concatenate(sine, axis=0).astype(BF16)

    tile(0, out_ref, 0)
    tile(1, out_ref, 256)

    @pl.when(third)
    def _():
        tile(2, out3_ref, 0)


def make_phases(where, lattice):
    return pl.pallas_call(
        phase_kernel,
        in_specs=[smem(), vmem()],
        out_specs=[vmem()] * 2,
        out_shape=[jax.ShapeDtypeStruct((POINTS, 512), BF16), jax.ShapeDtypeStruct((POINTS, 256), BF16)],
        scratch_shapes=[pltpu.VMEM((8, RW), jnp.int32)],
        compiler_params=pltpu.CompilerParams(vmem_limit_bytes=VMEM_LIMIT),
        cost_estimate=pl.CostEstimate(flops=1_500_000_000, bytes_accessed=3_000_000, transcendentals=0),
        name="phases",
    )(where, lattice)


def strength_kernel(groups, table_ref, lattice_ref, *refs):
    pays = refs[: 4 * groups]
    ph_ref, ph3_ref, s_ref, off_ref, mixed_ref, g_ref, w_ref, wide_ref = refs[4 * groups :]
    for slot in range(groups * QG):
        ref = pays[slot // 2]
        start = (slot % 2) * PAY
        group, inner = slot // QG, slot % QG
        for part in range(2):
            for mode in range(NM):
                source = start + part * CH + mode * 16
                mixed_ref[group, part, mode * 128 + inner * 16 : mode * 128 + inner * 16 + 16, :] = ref[source : source + 16, :]
        line = ref[start + 2 * CH : start + 2 * CH + 16, :128].astype(F32)[:8]
        small = line if inner == 0 else jnp.where(iota((8, 128), 1) >> 4 == inner, line, small)
        if inner == QG - 1:
            off_ref[group] = small.astype(jnp.int32)
            level = jnp.where(iota((NBIN, 128), 0) == small[:1].astype(jnp.int32), 1.0, 0.0).astype(BF16)
            table = table_ref[...]
            weights = None
            for _ in range(3):
                piece = table.astype(BF16)
                table = table - piece.astype(F32)
                got = jnp.dot(piece, level, preferred_element_type=F32)
                weights = got if weights is None else weights + got
            w_ref[group, :NM, :] = weights
    place, third, wide = order(widen(lattice_ref, wide_ref))
    general = third | wide

    def fill(first, count):
        span = count * 128
        rows = place[first * 128 : first * 128 + span]
        both = (((1,), (1,)), ((), ()))
        for group in range(groups):
            real = lax.dot_general(rows, mixed_ref[group, 0], both, preferred_element_type=F32)
            imag = lax.dot_general(rows, mixed_ref[group, 1], both, preferred_element_type=F32)
            minus = (-imag).astype(BF16)
            real = real.astype(BF16)
            imag = imag.astype(BF16)
            for t in range(count):
                here = slice(t * 128, (t + 1) * 128)
                low = (first + t) * 256
                for mode in range(NM):
                    lanes = slice(mode * 128, (mode + 1) * 128)
                    left = slice(mode * 256, mode * 256 + 128)
                    right = slice(mode * 256 + 128, mode * 256 + 256)
                    g_ref[group, low : low + 128, left] = real[here, lanes]
                    g_ref[group, low : low + 128, right] = imag[here, lanes]
                    g_ref[group, low + 128 : low + 256, left] = minus[here, lanes]
                    g_ref[group, low + 128 : low + 256, right] = real[here, lanes]

    fill(0, 2)
    pl.when(third)(lambda: fill(2, 1))

    def square(x):
        return x[:, :128] * x[:, :128] + x[:, 128:] * x[:, 128:]

    def run(full):
        sign = jnp.where(wide, 1.0, -1.0)

        def body(step, carry):
            rows = pl.ds(pl.multiple_of(step * STEP, STEP), STEP)
            for group in range(groups):
                plus = minus = None
                for mode in range(NM):
                    cols = slice(mode * 256, (mode + 1) * 256)
                    one = jnp.dot(ph_ref[rows, :256], g_ref[group, :256, cols], preferred_element_type=F32)
                    two = jnp.dot(ph_ref[rows, 256:], g_ref[group, 256:512, cols], preferred_element_type=F32)
                    if full:
                        three = jnp.dot(ph3_ref[rows, :], g_ref[group, 512:, cols], preferred_element_type=F32)
                        three = jnp.where(third, three, 0.0)
                        sums, differences = one + two + three, one + sign * two - three
                    else:
                        sums, differences = one + two, one - two
                    weight = w_ref[group, mode : mode + 1, :]
                    up, down = square(sums) * weight, square(differences) * weight
                    plus = up if plus is None else plus + up
                    minus = down if minus is None else minus + down
                s_ref[0, rows, group * 128 : (group + 1) * 128] = plus
                s_ref[1, rows, group * 128 : (group + 1) * 128] = minus
            return carry

        lax.fori_loop(0, POINTS // STEP, body, 0)

    pl.when(jnp.logical_not(general))(lambda: run(False))
    pl.when(general)(lambda: run(True))


def strengths(table, lattice, pays, phases, phases3, cost):
    groups = len(pays) // 4
    return pl.pallas_call(
        functools.partial(strength_kernel, groups),
        in_specs=[vmem()] * (4 + len(pays)),
        out_specs=[vmem()] * 2,
        out_shape=[
            jax.ShapeDtypeStruct((2, POINTS, groups * 128), F32),
            jax.ShapeDtypeStruct((groups, 8, 128), jnp.int32),
        ],
        scratch_shapes=[
            pltpu.VMEM((groups, 2, NM * 128, RW), BF16),
            pltpu.VMEM((groups, 768, 2 * NM * 128), BF16),
            pltpu.VMEM((groups, 8, 128), F32),
            pltpu.VMEM((8, RW), jnp.int32),
        ],
        compiler_params=pltpu.CompilerParams(vmem_limit_bytes=VMEM_LIMIT),
        cost_estimate=pl.CostEstimate(flops=cost, bytes_accessed=1000, transcendentals=0),
        name="strengths",
    )(table, lattice, *pays, phases, phases3)


def final_kernel(where_ref, off_a_ref, off_b_ref, own, *refs):
    parts = refs[: 2 * PARTS]
    sa_ref, sb_ref, out_ref, v_ref, arr_ref, off_ref, sem = refs[2 * PARTS :]
    slab = where_ref[0]
    core = where_ref[1]
    share = where_ref[2]
    copies = [
        pltpu.make_async_copy(off_a_ref.at[0], off_ref.at[0], sem.at[0]),
        pltpu.make_async_copy(off_b_ref.at[0], off_ref.at[1], sem.at[1]),
    ]

    def bring(src, plane, count):
        dst = v_ref.at[pl.ds(plane, count)]
        copies.append(pltpu.make_async_copy(src, dst.at[:, :, FRONT : FRONT + KX * KY], sem.at[len(copies)]))
        copies.append(pltpu.make_async_copy(src.at[:, :, :BACK], dst.at[:, :, FRONT + KX * KY :], sem.at[len(copies)]))
        copies.append(pltpu.make_async_copy(src.at[:, :, KX * KY - FRONT :], dst.at[:, :, :FRONT], sem.at[len(copies)]))

    bring(own, slab * PLANES, PLANES)
    for index in range(PARTS):
        for which in range(parts[index].shape[0]):
            source = where_ref[3 + WHICH[index] + which]
            bring(parts[index].at[which], source * PLANES + core * HP, HP)
            bring(parts[PARTS + index].at[which], source * PLANES + (1 - core) * HP, HP)
    for copy in copies:
        copy.start()

    ky = lax.rem(iota((NB, 512), 1), KY)
    row = iota((80, 256), 0)
    col = iota((80, 256), 1)
    gain = (row < 64) & (row >> 2 == col >> 4) & (row & 3 == col & 3)
    loss = (row >= 64) & (row - 64 == (col >> 2) & 3)
    spread = (jnp.where(gain, 1.0, 0.0) - jnp.where(loss, 1.0, 0.0)).astype(BF16)
    pick = jnp.where((iota((8, 128), 1) >> 2) & 3 == iota((8, 128), 0), 1.0, 0.0).astype(BF16)
    home = pl.multiple_of(((share * SHARE + FRONT) >> 7) * 128, 128)
    turn = lax.rem(WIN - lax.rem(share * SHARE, 128), WIN)
    arr_ref[:, 64:80, :] = jnp.zeros((UNROLL, 16, 512), F32)
    for copy in copies:
        copy.wait()

    def shift(step, lane):
        for slot in range(2 * QG):
            base = (slot % QG) * 16
            qx = off_ref[slot // QG, 1, base]
            qy = off_ref[slot // QG, 1, base + 1]
            qz = off_ref[slot // QG, 1, base + 2]
            plane = wrap(slab * PLANES + step + qz, KZ)
            first = wrap(share * ROWS + qx, KX) * KY
            start = first + qy + (FRONT - KY)
            aligned = pl.multiple_of((start >> 7) * 128, 128)
            window = v_ref[plane, :, pl.ds(aligned, WIN)].astype(F32)
            late = pltpu.roll(window, wrap(WIN - (start - aligned), WIN), 1)
            early = pltpu.roll(late, WIN - KY, 1)
            arr_ref[lane, NB * slot : NB * (slot + 1), :] = jnp.where(ky + qy < KY, early[:, :512], late[:, :512])
        window = v_ref[slab * PLANES + step, :, pl.ds(home, WIN)].astype(F32)
        arr_ref[lane, 64:68, :] = pltpu.roll(window, turn, 1)[:, :512]

    def combine(step, lane):
        arrived = arr_ref[lane].astype(BF16)
        diff = lax.dot_general(arrived, spread, (((0,), (0,)), ((), ())), preferred_element_type=F32)
        terms = []
        for kx in range(ROWS):
            for upper in range(2):
                rows = pl.ds(pl.multiple_of((step * ROWS + kx) * HALF, HALF), HALF)
                here = slice((2 * kx + upper) * HALF, (2 * kx + upper + 1) * HALF)
                terms.append(sa_ref[upper, rows, :] * diff[here, :128] + sb_ref[upper, rows, :] * diff[here, 128:])
        term = jnp.concatenate(terms, axis=0)
        result = None
        for _ in range(3):
            piece = term.astype(BF16)
            term = term - piece.astype(F32)
            got = lax.dot_general(pick, piece, (((1,), (1,)), ((), ())), preferred_element_type=F32)
            result = got if result is None else result + got
        out_ref[step] = result[:NB] * (1.0 / (2 * QG * NM))

    def body(step, carry):
        for lane in range(UNROLL):
            shift(step * UNROLL + lane, lane)
        for lane in range(UNROLL):
            combine(step * UNROLL + lane, lane)
        return carry

    lax.fori_loop(0, PLANES // UNROLL, body, 0)


def contract(where, off_a, off_b, own, parts, s_a, s_b):
    return pl.pallas_call(
        final_kernel,
        in_specs=[smem()] + [anywhere()] * (3 + 2 * PARTS) + [vmem()] * 2,
        out_specs=vmem(),
        out_shape=jax.ShapeDtypeStruct((PLANES, NB, SHARE), F32),
        scratch_shapes=[
            pltpu.VMEM((KZ, NB, VLANES), BF16),
            pltpu.VMEM((UNROLL, 80, 512), F32),
            pltpu.SMEM((2, 8, 128), jnp.int32),
            pltpu.SemaphoreType.DMA((47,)),
        ],
        compiler_params=pltpu.CompilerParams(vmem_limit_bytes=VMEM_LIMIT),
        cost_estimate=pl.CostEstimate(flops=2_000_000_000, bytes_accessed=9_000_000, transcendentals=0),
        name="contract",
    )(where, off_a, off_b, own, *parts, s_a, s_b)


def local(occupation, q_offsets, coupling, window_bins, lorentz_table, lattice):
    slab = lax.axis_index("ka")
    share = lax.axis_index("pb")
    core = share % 2

    def place(ylo, x, z, yhi, c):
        return ((ylo * 4 + x) * 16) + z * 4 + yhi * 2 + c

    def move(array, to):
        grid = [(yl, x, z, yh, c) for yl in range(2) for x in range(4) for z in range(4) for yh in range(2) for c in range(2)]
        return lax.ppermute(array, ("ka", "pb"), [(place(*at), place(*to(*at))) for at in grid])

    def core_swap(array):
        return move(array, lambda yl, x, z, yh, c: (yl, x, z, yh, 1 - c))

    tie = lax.optimization_barrier
    half = lax.dynamic_slice_in_dim(occupation, core * HP, HP, 0)[None]
    beyond = move(half, lambda yl, x, z, yh, c: (1 - yl, x, z, yh, c))
    pay = pack(q_offsets, window_bins, jnp.swapaxes(coupling[0], 1, 2))
    early2 = move(half, lambda yl, x, z, yh, c: (yl, (x + 2) % 4, z, yh, c))
    twin = move(pay, lambda yl, x, z, yh, c: (1 - yl, x, z, 1 - yh, c))
    ylo, x = slab // 4, slab % 4
    lines = [(1, 0), (0, 2), (0, 1), (1, 1), (0, 3), (1, 3), (1, 2)]
    sources = [(ylo if y == 0 else 1 - ylo) * 4 + (x + 4 - d) % 4 for y, d in lines]
    where = jnp.stack([slab, core, share] + sources).astype(jnp.int32)
    both = jnp.concatenate([half, beyond], axis=0)
    phases, phases3 = make_phases(where, lattice)
    twin, both, phases, phases3, early2 = tie((twin, both, phases, phases3, early2))
    pair = jnp.concatenate([pay, twin], axis=0)
    group = [pair] + [move(pair, lambda yl, x, z, yh, c: (yl, x, (z + d) % 4, yh, c)) for d in (1, 3, 2)]
    late1 = move(both, lambda yl, x, z, yh, c: (yl, (x + 1) % 4, z, yh, c))
    late3 = move(both, lambda yl, x, z, yh, c: (yl, (x + 3) % 4, z, yh, c))
    late2 = move(beyond, lambda yl, x, z, yh, c: (yl, (x + 2) % 4, z, yh, c))
    table = lorentz_table.T
    first = [group[0], core_swap(group[0]), group[1], core_swap(group[1])]
    s_a, off_a = strengths(table, lattice, first, phases, phases3, 1000)
    phases, s_a = tie((phases, s_a))
    second = [group[2], core_swap(group[2]), group[3], core_swap(group[3])]
    s_b, off_b = strengths(table, lattice, second, phases, phases3, 1000)
    late1, late3, late2, s_a = tie((late1, late3, late2, s_a))
    fetched = [beyond, early2, late1, late3, late2]
    swapped = [core_swap(array) for array in fetched]
    return contract(where, off_a, off_b, occupation, fetched + swapped, s_a, s_b)


def solution(mesh):
    in_specs = (
        P("ka", None, None),
        P("pb", None),
        P("pb", None, None, None),
        P("pb", None),
        P(),
        P(),
    )
    out_specs = P("ka", None, "pb")
    return jax.shard_map(local, mesh=mesh, in_specs=in_specs, out_specs=out_specs, check_vma=False)
```

```python
import functools
import math

import jax
import jax.numpy as jnp
from jax import lax
from jax.experimental import pallas as pl
from jax.experimental.pallas import tpu as pltpu
from jax.sharding import PartitionSpec as P

KX = 80
KY = 80
KZ = 80
NB = 4
NM = 6
NR = 200
RW = 256
CH = 96
NBIN = 32
QG = 8
PLANES = 10
HP = PLANES // 2
PARTS = 5
WHICH = (0, 1, 2, 4, 6)
ROWS = 5
HALF = KY // 2
SHARE = ROWS * KY
POINTS = PLANES * ROWS * HALF
PAY = 2 * CH + 16
SLOTS = 384
FRONT = 128
BACK = 512
VLANES = FRONT + KX * KY + BACK
WIN = 640
STEP = 1000
UNROLL = 10
VMEM_LIMIT = 20 * 1024 * 1024
F32 = jnp.float32
BF16 = jnp.bfloat16


def smem():
    return pl.BlockSpec(memory_space=pltpu.SMEM)


def vmem():
    return pl.BlockSpec(memory_space=pltpu.VMEM)


def anywhere():
    return pl.BlockSpec(memory_space=pl.ANY)


def wrap(value, size):
    return jnp.where(value >= size, value - size, value)


def iota(shape, axis):
    return lax.broadcasted_iota(jnp.int32, shape, axis)


def pack_kernel(off_ref, bins_ref, coupling_ref, pay_ref):
    row = iota((CH, CH), 0)
    moved = jnp.where(iota((CH, CH), 1) == (row & 15) * NM + (row >> 4), 1.0, 0.0).astype(BF16)
    pay_ref[:, NR:] = jnp.zeros((PAY, RW - NR), BF16)
    for part in range(2):
        block = jnp.dot(moved, coupling_ref[part], preferred_element_type=F32)
        pay_ref[part * CH : (part + 1) * CH, :NR] = block.astype(BF16)
    lane = iota((16, 128), 1) & 15
    line = iota((16, 128), 0)
    small = jnp.zeros((16, 128), F32)
    for pair in range(NB * NB):
        small = jnp.where((line == 0) & (lane == pair), bins_ref[0, pair].astype(F32), small)
    for axis in range(3):
        small = jnp.where((line == 1) & (lane == axis), off_ref[0, axis].astype(F32), small)
    pay_ref[2 * CH :, :128] = small.astype(BF16)
    pay_ref[2 * CH :, 128:] = jnp.zeros((16, RW - 128), BF16)


def pack(q_offsets, window_bins, coupling):
    return pl.pallas_call(
        pack_kernel,
        in_specs=[smem(), smem(), vmem()],
        out_specs=vmem(),
        out_shape=jax.ShapeDtypeStruct((PAY, RW), BF16),
        name="pack",
    )(q_offsets, window_bins, coupling)


def sine_of(turns):
    x = turns * (math.pi / 40)
    y = x * x
    s = -2.3889859e-08
    for c in (2.7525562e-06, -1.9840874e-04, 8.3333310e-03, -1.6666667e-01, 1.0):
        s = s * y + c
    return x * s


def cos_sin(steps):
    t = steps - 80.0 * jnp.round(steps * (1.0 / 80.0))
    a = jnp.abs(t)
    cosine = sine_of(20.0 - a)
    folded = jnp.where(a > 20.0, 40.0 - a, a)
    sine = sine_of(jnp.where(t < 0.0, -folded, folded))
    return cosine, sine


def order(lattice):
    lane = iota((8, 256), 1)
    even = jnp.where((jnp.broadcast_to(lattice[1:2, :], (8, 256)) & 1) == 0, 1, 0)
    real = lane < NR
    is_even = jnp.where(real, even, 0).astype(BF16)
    before = jnp.where(iota((256, 256), 0) < iota((256, 256), 1), 1.0, 0.0).astype(BF16)
    rank = jnp.dot(is_even, before, preferred_element_type=F32).astype(jnp.int32)
    count = jnp.sum(is_even[:1].astype(F32), axis=1, keepdims=True).astype(jnp.int32)
    base = jnp.where(count > 128, 256, 128)
    slot = jnp.where(even == 1, rank, lane - rank + base)
    slot = jnp.where(real, slot, -1)[:1]
    count = count[0, 0]
    wide = count > 128
    third = (wide & (count < NR)) | (count < NR - 128)
    place = jnp.where(iota((SLOTS, 256), 0) == slot, 1.0, 0.0).astype(BF16)
    return place, third, wide


def widen(lattice_ref, wide_ref):
    wide_ref[...] = jnp.zeros((8, RW), jnp.int32)
    wide_ref[:3, :NR] = lattice_ref[...]
    return wide_ref[...]


def phase_kernel(where_ref, lattice_ref, out_ref, out3_ref, wide_ref):
    lattice = widen(lattice_ref, wide_ref)
    place, third, _ = order(lattice)
    vectors = lax.dot_general(lattice.astype(BF16), place, (((1,), (1,)), ((), ())), preferred_element_type=F32)
    n = PLANES * ROWS
    row = iota((56, SLOTS), 0)
    upper = (row * 52) >> 8
    kz = (where_ref[0] * PLANES + upper).astype(F32)
    kx = (where_ref[2] * ROWS + row - ROWS * upper).astype(F32)
    ac, an = cos_sin(kx * vectors[0:1] + kz * vectors[2:3])
    ky = iota((HALF, SLOTS), 0).astype(F32)
    bc, bs = cos_sin(ky * vectors[1:2])

    def tile(t, ref, lane):
        cols = slice(t * 128, (t + 1) * 128)
        c, s = bc[:, cols], bs[:, cols]
        for r in range(0, n, 2):
            cosine, sine = [], []
            for k in (r, r + 1):
                u, v = ac[k : k + 1, cols], an[k : k + 1, cols]
                cosine.append(u * c - v * s)
                sine.append(v * c + u * s)
            rows = slice(r * HALF, (r + 2) * HALF)
            ref[rows, lane : lane + 128] = jnp.concatenate(cosine, axis=0).astype(BF16)
            ref[rows, lane + 128 : lane + 256] = jnp.concatenate(sine, axis=0).astype(BF16)

    tile(0, out_ref, 0)
    tile(1, out_ref, 256)

    @pl.when(third)
    def _():
        tile(2, out3_ref, 0)


def make_phases(where, lattice):
    return pl.pallas_call(
        phase_kernel,
        in_specs=[smem(), vmem()],
        out_specs=[vmem()] * 2,
        out_shape=[jax.ShapeDtypeStruct((POINTS, 512), BF16), jax.ShapeDtypeStruct((POINTS, 256), BF16)],
        scratch_shapes=[pltpu.VMEM((8, RW), jnp.int32)],
        compiler_params=pltpu.CompilerParams(vmem_limit_bytes=VMEM_LIMIT),
        cost_estimate=pl.CostEstimate(flops=1_500_000_000, bytes_accessed=3_000_000, transcendentals=0),
        name="phases",
    )(where, lattice)


def strength_kernel(groups, table_ref, lattice_ref, *refs):
    pays = refs[: 4 * groups]
    ph_ref, ph3_ref, s_ref, off_ref, mixed_ref, g_ref, w_ref, wide_ref = refs[4 * groups :]
    for slot in range(groups * QG):
        ref = pays[slot // 2]
        start = (slot % 2) * PAY
        group, inner = slot // QG, slot % QG
        for part in range(2):
            for mode in range(NM):
                source = start + part * CH + mode * 16
                mixed_ref[group, part, mode * 128 + inner * 16 : mode * 128 + inner * 16 + 16, :] = ref[source : source + 16, :]
        line = ref[start + 2 * CH : start + 2 * CH + 16, :128].astype(F32)[:8]
        small = line if inner == 0 else jnp.where(iota((8, 128), 1) >> 4 == inner, line, small)
        if inner == QG - 1:
            off_ref[group] = small.astype(jnp.int32)
            level = jnp.where(iota((NBIN, 128), 0) == small[:1].astype(jnp.int32), 1.0, 0.0).astype(BF16)
            table = table_ref[...]
            weights = None
            for _ in range(3):
                piece = table.astype(BF16)
                table = table - piece.astype(F32)
                got = jnp.dot(piece, level, preferred_element_type=F32)
                weights = got if weights is None else weights + got
            w_ref[group, :NM, :] = weights
    place, third, wide = order(widen(lattice_ref, wide_ref))
    general = third | wide

    def fill(first, count):
        span = count * 128
        rows = place[first * 128 : first * 128 + span]
        both = (((1,), (1,)), ((), ()))
        for group in range(groups):
            real = lax.dot_general(rows, mixed_ref[group, 0], both, preferred_element_type=F32)
            imag = lax.dot_general(rows, mixed_ref[group, 1], both, preferred_element_type=F32)
            minus = (-imag).astype(BF16)
            real = real.astype(BF16)
            imag = imag.astype(BF16)
            for t in range(count):
                here = slice(t * 128, (t + 1) * 128)
                low = (first + t) * 256
                for mode in range(NM):
                    lanes = slice(mode * 128, (mode + 1) * 128)
                    left = slice(mode * 256, mode * 256 + 128)
                    right = slice(mode * 256 + 128, mode * 256 + 256)
                    g_ref[group, low : low + 128, left] = real[here, lanes]
                    g_ref[group, low : low + 128, right] = imag[here, lanes]
                    g_ref[group, low + 128 : low + 256, left] = minus[here, lanes]
                    g_ref[group, low + 128 : low + 256, right] = real[here, lanes]

    fill(0, 2)
    pl.when(third)(lambda: fill(2, 1))

    def square(x):
        return x[:, :128] * x[:, :128] + x[:, 128:] * x[:, 128:]

    def run(full):
        sign = jnp.where(wide, 1.0, -1.0)

        def body(step, carry):
            rows = pl.ds(pl.multiple_of(step * STEP, STEP), STEP)
            for group in range(groups):
                plus = minus = None
                for mode in range(NM):
                    cols = slice(mode * 256, (mode + 1) * 256)
                    one = jnp.dot(ph_ref[rows, :256], g_ref[group, :256, cols], preferred_element_type=F32)
                    two = jnp.dot(ph_ref[rows, 256:], g_ref[group, 256:512, cols], preferred_element_type=F32)
                    if full:
                        three = jnp.dot(ph3_ref[rows, :], g_ref[group, 512:, cols], preferred_element_type=F32)
                        three = jnp.where(third, three, 0.0)
                        sums, differences = one + two + three, one + sign * two - three
                    else:
                        sums, differences = one + two, one - two
                    weight = w_ref[group, mode : mode + 1, :]
                    up, down = square(sums) * weight, square(differences) * weight
                    plus = up if plus is None else plus + up
                    minus = down if minus is None else minus + down
                s_ref[0, rows, group * 128 : (group + 1) * 128] = plus
                s_ref[1, rows, group * 128 : (group + 1) * 128] = minus
            return carry

        lax.fori_loop(0, POINTS // STEP, body, 0)

    pl.when(jnp.logical_not(general))(lambda: run(False))
    pl.when(general)(lambda: run(True))


def strengths(table, lattice, pays, phases, phases3, cost):
    groups = len(pays) // 4
    return pl.pallas_call(
        functools.partial(strength_kernel, groups),
        in_specs=[vmem()] * (4 + len(pays)),
        out_specs=[vmem()] * 2,
        out_shape=[
            jax.ShapeDtypeStruct((2, POINTS, groups * 128), F32),
            jax.ShapeDtypeStruct((groups, 8, 128), jnp.int32),
        ],
        scratch_shapes=[
            pltpu.VMEM((groups, 2, NM * 128, RW), BF16),
            pltpu.VMEM((groups, 768, 2 * NM * 128), BF16),
            pltpu.VMEM((groups, 8, 128), F32),
            pltpu.VMEM((8, RW), jnp.int32),
        ],
        compiler_params=pltpu.CompilerParams(vmem_limit_bytes=VMEM_LIMIT),
        cost_estimate=pl.CostEstimate(flops=cost, bytes_accessed=1000, transcendentals=0),
        name="strengths",
    )(table, lattice, *pays, phases, phases3)


def final_kernel(where_ref, off_a_ref, off_b_ref, own, *refs):
    parts = refs[: 2 * PARTS]
    sa_ref, sb_ref, out_ref, v_ref, arr_ref, off_ref, sem = refs[2 * PARTS :]
    slab = where_ref[0]
    core = where_ref[1]
    share = where_ref[2]
    copies = [
        pltpu.make_async_copy(off_a_ref.at[0], off_ref.at[0], sem.at[0]),
        pltpu.make_async_copy(off_b_ref.at[0], off_ref.at[1], sem.at[1]),
    ]

    def bring(src, plane, count):
        dst = v_ref.at[pl.ds(plane, count)]
        copies.append(pltpu.make_async_copy(src, dst.at[:, :, FRONT : FRONT + KX * KY], sem.at[len(copies)]))
        copies.append(pltpu.make_async_copy(src.at[:, :, :BACK], dst.at[:, :, FRONT + KX * KY :], sem.at[len(copies)]))
        copies.append(pltpu.make_async_copy(src.at[:, :, KX * KY - FRONT :], dst.at[:, :, :FRONT], sem.at[len(copies)]))

    bring(own, slab * PLANES, PLANES)
    for index in range(PARTS):
        for which in range(parts[index].shape[0]):
            source = where_ref[3 + WHICH[index] + which]
            bring(parts[index].at[which], source * PLANES + core * HP, HP)
            bring(parts[PARTS + index].at[which], source * PLANES + (1 - core) * HP, HP)
    for copy in copies:
        copy.start()

    ky = lax.rem(iota((NB, 512), 1), KY)
    row = iota((80, 256), 0)
    col = iota((80, 256), 1)
    gain = (row < 64) & (row >> 2 == col >> 4) & (row & 3 == col & 3)
    loss = (row >= 64) & (row - 64 == (col >> 2) & 3)
    spread = (jnp.where(gain, 1.0, 0.0) - jnp.where(loss, 1.0, 0.0)).astype(BF16)
    pick = jnp.where((iota((8, 128), 1) >> 2) & 3 == iota((8, 128), 0), 1.0, 0.0).astype(BF16)
    home = pl.multiple_of(((share * SHARE + FRONT) >> 7) * 128, 128)
    turn = lax.rem(WIN - lax.rem(share * SHARE, 128), WIN)
    arr_ref[:, 64:80, :] = jnp.zeros((UNROLL, 16, 512), F32)
    for copy in copies:
        copy.wait()

    def shift(step, lane):
        for slot in range(2 * QG):
            base = (slot % QG) * 16
            qx = off_ref[slot // QG, 1, base]
            qy = off_ref[slot // QG, 1, base + 1]
            qz = off_ref[slot // QG, 1, base + 2]
            plane = wrap(slab * PLANES + step + qz, KZ)
            first = wrap(share * ROWS + qx, KX) * KY
            start = first + qy + (FRONT - KY)
            aligned = pl.multiple_of((start >> 7) * 128, 128)
            window = v_ref[plane, :, pl.ds(aligned, WIN)].astype(F32)
            late = pltpu.roll(window, wrap(WIN - (start - aligned), WIN), 1)
            early = pltpu.roll(late, WIN - KY, 1)
            arr_ref[lane, NB * slot : NB * (slot + 1), :] = jnp.where(ky + qy < KY, early[:, :512], late[:, :512])
        window = v_ref[slab * PLANES + step, :, pl.ds(home, WIN)].astype(F32)
        arr_ref[lane, 64:68, :] = pltpu.roll(window, turn, 1)[:, :512]

    def combine(step, lane):
        arrived = arr_ref[lane].astype(BF16)
        diff = lax.dot_general(arrived, spread, (((0,), (0,)), ((), ())), preferred_element_type=F32)
        terms = []
        for kx in range(ROWS):
            for upper in range(2):
                rows = pl.ds(pl.multiple_of((step * ROWS + kx) * HALF, HALF), HALF)
                here = slice((2 * kx + upper) * HALF, (2 * kx + upper + 1) * HALF)
                terms.append(sa_ref[upper, rows, :] * diff[here, :128] + sb_ref[upper, rows, :] * diff[here, 128:])
        term = jnp.concatenate(terms, axis=0)
        result = None
        for _ in range(3):
            piece = term.astype(BF16)
            term = term - piece.astype(F32)
            got = lax.dot_general(pick, piece, (((1,), (1,)), ((), ())), preferred_element_type=F32)
            result = got if result is None else result + got
        out_ref[step] = result[:NB] * (1.0 / (2 * QG * NM))

    def body(step, carry):
        for lane in range(UNROLL):
            shift(step * UNROLL + lane, lane)
        for lane in range(UNROLL):
            combine(step * UNROLL + lane, lane)
        return carry

    lax.fori_loop(0, PLANES // UNROLL, body, 0)


def contract(where, off_a, off_b, own, parts, s_a, s_b):
    return pl.pallas_call(
        final_kernel,
        in_specs=[smem()] + [anywhere()] * (3 + 2 * PARTS) + [vmem()] * 2,
        out_specs=vmem(),
        out_shape=jax.ShapeDtypeStruct((PLANES, NB, SHARE), F32),
        scratch_shapes=[
            pltpu.VMEM((KZ, NB, VLANES), BF16),
            pltpu.VMEM((UNROLL, 80, 512), F32),
            pltpu.SMEM((2, 8, 128), jnp.int32),
            pltpu.SemaphoreType.DMA((47,)),
        ],
        compiler_params=pltpu.CompilerParams(vmem_limit_bytes=VMEM_LIMIT),
        cost_estimate=pl.CostEstimate(flops=2_000_000_000, bytes_accessed=9_000_000, transcendentals=0),
        name="contract",
    )(where, off_a, off_b, own, *parts, s_a, s_b)


def local(occupation, q_offsets, coupling, window_bins, lorentz_table, lattice):
    slab = lax.axis_index("ka")
    share = lax.axis_index("pb")
    core = share % 2

    def place(ylo, x, z, yhi, c):
        return ((ylo * 4 + x) * 16) + z * 4 + yhi * 2 + c

    def move(array, to):
        grid = [(yl, x, z, yh, c) for yl in range(2) for x in range(4) for z in range(4) for yh in range(2) for c in range(2)]
        return lax.ppermute(array, ("ka", "pb"), [(place(*at), place(*to(*at))) for at in grid])

    def core_swap(array):
        return move(array, lambda yl, x, z, yh, c: (yl, x, z, yh, 1 - c))

    tie = lax.optimization_barrier
    half = lax.dynamic_slice_in_dim(occupation, core * HP, HP, 0)[None]
    beyond = move(half, lambda yl, x, z, yh, c: (1 - yl, x, z, yh, c))
    pay = pack(q_offsets, window_bins, jnp.swapaxes(coupling[0], 1, 2))
    early2 = move(half, lambda yl, x, z, yh, c: (yl, (x + 2) % 4, z, yh, c))
    twin = move(pay, lambda yl, x, z, yh, c: (1 - yl, x, z, 1 - yh, c))
    ylo, x = slab // 4, slab % 4
    lines = [(1, 0), (0, 2), (0, 1), (1, 1), (0, 3), (1, 3), (1, 2)]
    sources = [(ylo if y == 0 else 1 - ylo) * 4 + (x + 4 - d) % 4 for y, d in lines]
    where = jnp.stack([slab, core, share] + sources).astype(jnp.int32)
    both = jnp.concatenate([half, beyond], axis=0)
    phases, phases3 = make_phases(where, lattice)
    twin, both, phases, phases3, early2 = tie((twin, both, phases, phases3, early2))
    pair = jnp.concatenate([pay, twin], axis=0)
    group = [pair] + [move(pair, lambda yl, x, z, yh, c: (yl, x, (z + d) % 4, yh, c)) for d in (1, 3, 2)]
    late1 = move(both, lambda yl, x, z, yh, c: (yl, (x + 1) % 4, z, yh, c))
    late3 = move(both, lambda yl, x, z, yh, c: (yl, (x + 3) % 4, z, yh, c))
    late2 = move(beyond, lambda yl, x, z, yh, c: (yl, (x + 2) % 4, z, yh, c))
    table = lorentz_table.T
    first = [group[0], core_swap(group[0]), group[1], core_swap(group[1])]
    s_a, off_a = strengths(table, lattice, first, phases, phases3, 1000)
    phases, s_a = tie((phases, s_a))
    second = [group[2], core_swap(group[2]), group[3], core_swap(group[3])]
    s_b, off_b = strengths(table, lattice, second, phases, phases3, 1000)
    late1, late3, late2, s_a = tie((late1, late3, late2, s_a))
    fetched = [beyond, early2, late1, late3, late2]
    swapped = [core_swap(array) for array in fetched]
    return contract(where, off_a, off_b, occupation, fetched + swapped, s_a, s_b)


def solution(mesh):
    in_specs = (
        P("ka", None, None),
        P("pb", None),
        P("pb", None, None, None),
        P("pb", None),
        P(),
        P(),
    )
    out_specs = P("ka", None, "pb")
    return jax.shard_map(local, mesh=mesh, in_specs=in_specs, out_specs=out_specs, check_vma=False)
```
